256 devices in a mesh: rows: 64 (over y, z, core), grp: 4 (over x).
Axes of the slice: x: 4, y: 4, z: 8, core: 2. Of those that a mesh axis runs over, the one named last changes fastest.
Arguments:
- sensitivity: bfloat16 [4, 1048576, 256], P('grp', 'rows')
- block_moves: int32 [4, 64, 4], P('grp', 'rows'), may hold values from 0 to 32, as said below
- shape_modes: bfloat16 [4, 524288, 128], P('grp', 'rows'), may hold values from -6 to 6
Outputs:
- factor: float32 [256, 256], replicated
- projection: float32 [128, 256], replicated
The draws below stay inside these ranges and needn't reach their ends.
Inputs may be any that keep to these rules, and one draw needn't show every extreme that they name: block_moves[g, d] = (h, t, p, n): device d holds 64 + h + t - p - n valid blocks in its first slots, in row order; its first h go to device d - 1 and its last t to device d + 1; p is the t of device d - 1 and n the h of device d + 1, both 0 where that device does not exist; of the t of device d and the h of device d + 1 at most one is nonzero; p + n <= 64.
All inputs are finite; a program needn't handle non-finite values.
Results may differ from the reference program's by a relative error of at most 0.00455.
The reference program's roundings to bfloat16 on the way count: a program that leaves them out, or rounds other values in their place, can miss the bound.
Values may be sent and summed in bfloat16 or wider, within the bound.
No kernel may reach another device: no remote copies, remote signals or barrier semaphores. Data moves between devices by JAX's collectives and lax.ppermute only.
A program may use at most 128 MiB of HBM per device.

```python
import math
import jax
import jax.numpy as jnp
from jax import lax

MEMBERS = 256
MODES = 128
BLOCK = 128
BLOCKS = 64
DRIFT = 32
SLOTS = 128
TOTAL_ROWS = 2097152
N_ROWS = 64
N_GRP = 4


def draw_sensitivity(key, part):
    first_key, second_key, factor_key, weight_key, spread_key = jax.random.split(key, 5)
    rows_here = N_ROWS * SLOTS * BLOCK
    full_shape = (N_GRP, rows_here, MEMBERS)
    position = (jnp.arange(N_GRP, dtype=jnp.float32)[:, None, None] * rows_here + jnp.arange(rows_here, dtype=jnp.float32)[None, :, None]) / (N_GRP * rows_here)
    row_spread = jnp.exp(jax.random.uniform(spread_key, (N_GRP, rows_here, 1), jnp.float32, 0.0, math.log(10.0)))
    row_scale = (1.0 + 2.0 * position) * row_spread * 0.3162278
    common = jax.random.normal(factor_key, (8, N_GRP, rows_here, 1), jnp.float32)
    base = jax.random.normal(first_key, full_shape, jnp.float32)
    column_scale = jnp.exp(jax.random.uniform(second_key, (MEMBERS,), jnp.float32, 0.0, math.log(10.0)))
    weights = jax.random.normal(weight_key, (8, MEMBERS), jnp.float32) * 0.6
    mixed = base + 0.7 * jnp.roll(base, -1, axis=2)
    for index in range(8):
        mixed = mixed + common[index] * weights[index][None, None, :]
    values = mixed * row_scale * column_scale[None, None, :] * float(TOTAL_ROWS) ** (-0.5)
    return values.astype(jnp.bfloat16)


def draw_block_moves(key, part):
    size_key, sign_key, place_key = jax.random.split(key, 3)
    bounds = N_ROWS - 1
    magnitude = jax.random.randint(size_key, (N_GRP, bounds), (DRIFT + 1) // 2, DRIFT + 1)
    sign_value = jax.random.randint(sign_key, (N_GRP, bounds), 0, 2) * 2 - 1
    shifts = magnitude * sign_value
    forced = jax.random.randint(place_key, (N_GRP, 1), 1, N_ROWS - 1)
    column = jnp.arange(bounds, dtype=jnp.int32)[None, :]
    shifts = jnp.where(column == forced - 1, DRIFT, jnp.where(column == forced, -DRIFT, shifts))
    zero_column = jnp.zeros((N_GRP, 1), jnp.int32)
    head_count = jnp.concatenate([zero_column, jnp.maximum(shifts, 0)], axis=1)
    tail_count = jnp.concatenate([jnp.maximum(-shifts, 0), zero_column], axis=1)
    prev_tail = jnp.concatenate([zero_column, tail_count[:, :-1]], axis=1)
    next_head = jnp.concatenate([head_count[:, 1:], zero_column], axis=1)
    return jnp.stack([head_count, tail_count, prev_tail, next_head], axis=-1).astype(jnp.int32)


def level_of(own_key, shape, pieces, smallest, largest):
    loudness = 1.0
    for dim, shards_of in pieces:
        steps = jax.random.uniform(jax.random.fold_in(jax.random.fold_in(own_key, 6), dim), (shards_of,), jnp.float32, smallest / len(pieces), largest / len(pieces))
        loudness = loudness * jnp.repeat(jnp.exp(steps), shape[dim] // shards_of).reshape((-1,) + (1,) * (len(shape) - 1 - dim))
    return loudness


def normal_values(rng, extent, scale, limit, cuts=(), kind=jnp.bfloat16):
    values = jax.random.normal(rng, extent, jnp.float32) * scale
    if len(cuts) > 0:
        values = level_of(rng, extent, cuts, -0.22, 0.18) * values
    return jnp.clip(values, min=-limit, max=limit).astype(kind)


def setup_inputs(seed: int = 0) -> dict:
    splits = jax.random.split(jax.random.key(seed), 4)
    return {
        "sensitivity": draw_sensitivity(jax.random.fold_in(splits[3], 71), 0),
        "block_moves": draw_block_moves(jax.random.fold_in(splits[3], 71), 0),
        "shape_modes": normal_values(splits[2], (N_GRP, N_ROWS * BLOCKS * BLOCK, MODES), 1.0, 6.0, ((0, 4), (1, 64))),
    }


def upper_factor(gram):
    size = gram.shape[0]
    columns = jnp.arange(size, dtype=jnp.int32)

    def step(k, carry):
        rest, factor = carry
        row = lax.dynamic_index_in_dim(rest, k, 0, keepdims=False)
        pivot = lax.dynamic_index_in_dim(row, k, 0, keepdims=False)
        row = jnp.where(columns >= k, row / jnp.sqrt(pivot), jnp.zeros_like(row))
        rest = rest - row[:, None] * row[None, :]
        factor = lax.dynamic_update_index_in_dim(factor, row, k, 0)
        return (rest, factor)
    result = lax.fori_loop(0, size, step, (gram, jnp.zeros_like(gram)))
    return result[1]

def upper_inverse(factor):
    size = factor.shape[0]
    columns = jnp.arange(size, dtype=jnp.int32)

    def step(i, result):
        k = size - 1 - i
        row = lax.dynamic_index_in_dim(factor, k, 0, keepdims=False)
        diag = lax.dynamic_index_in_dim(row, k, 0, keepdims=False)
        beyond = jnp.where(columns > k, row, jnp.zeros_like(row))
        unit = jnp.where(columns == k, jnp.ones_like(row), jnp.zeros_like(row))
        fresh = (unit - jnp.dot(beyond, result, precision=lax.Precision.HIGHEST)) / diag
        return lax.dynamic_update_index_in_dim(result, fresh, k, 0)
    return lax.fori_loop(0, size, step, jnp.zeros_like(factor))

def balance(blocks, moves_group):
    head_count = moves_group[:, 0].astype(jnp.int32)
    prev_tail = moves_group[:, 2].astype(jnp.int32)
    next_head = moves_group[:, 3].astype(jnp.int32)
    own_count = (BLOCKS - prev_tail - next_head).astype(jnp.int32)
    device = jnp.arange(N_ROWS, dtype=jnp.int32)[:, None]
    target = jnp.arange(BLOCKS, dtype=jnp.int32)[None, :]
    start_prev = jnp.concatenate([jnp.zeros((1,), jnp.int32), (head_count + own_count)[:-1]]).astype(jnp.int32)
    first = target < prev_tail[:, None]
    middle = target < (prev_tail + own_count)[:, None]
    source_dev = jnp.where(first, device - 1, jnp.where(middle, device, device + 1))
    source_slot = jnp.where(first, start_prev[:, None] + target, jnp.where(middle, head_count[:, None] + target - prev_tail[:, None], target - (prev_tail + own_count)[:, None]))
    source_dev = jnp.clip(source_dev, 0, N_ROWS - 1).astype(jnp.int32)
    source_slot = jnp.clip(source_slot, 0, SLOTS - 1).astype(jnp.int32)
    return blocks[source_dev, source_slot]

def group_rows(sensitivity, block_moves, group):
    blocks = sensitivity[group].reshape(N_ROWS, SLOTS, BLOCK, MEMBERS)
    return balance(blocks, block_moves[group]).reshape(-1, MEMBERS)

def reference(sensitivity, block_moves, shape_modes):
    gram = jnp.zeros((MEMBERS, MEMBERS), jnp.float32)
    for group in range(N_GRP):
        panel_rows = group_rows(sensitivity, block_moves, group)
        gram = gram + jnp.dot(panel_rows.T, panel_rows, preferred_element_type=jnp.float32)
    factor = upper_factor(gram)
    inverse = upper_inverse(factor).astype(jnp.bfloat16)
    projection = jnp.zeros((MODES, MEMBERS), jnp.float32)
    for group in range(N_GRP):
        panel_rows = group_rows(sensitivity, block_moves, group)
        ortho_rows = jnp.dot(panel_rows, inverse, preferred_element_type=jnp.float32).astype(jnp.bfloat16)
        projection = projection + jnp.dot(shape_modes[group].T, ortho_rows, preferred_element_type=jnp.float32)
    return (factor, projection)
```

```python
import jax
import jax.numpy as jnp
from jax import lax
from jax.experimental import pallas as pl
from jax.experimental.pallas import tpu as pltpu
from jax.sharding import Mesh, PartitionSpec as P

BLOCK = 128
LANES = 128
MEMBERS = 256
MODES = 128
CHUNK = 8
CHUNK_ROWS = CHUNK * BLOCK
TILE = 8
STACK = 768


def transposed_product(a, b):
    return lax.dot_general(a, b, (((0,), (0,)), ((), ())), preferred_element_type=jnp.float32)


def kept_rows(values, first, start, stop):
    row = first + lax.broadcasted_iota(jnp.int32, values.shape, 0)
    keep = (row >= start) & (row < stop)
    return jnp.where(keep, values, jnp.zeros_like(values))


def own_rows_kernel(moves, panel, modes, out, panel_v, modes_v, gram, cross, panel_sem, modes_sem):
    head, tail, prev, following = moves[0], moves[1], moves[2], moves[3]
    block_total = modes.shape[0] // BLOCK
    lead = block_total // 2
    own = block_total - prev - following
    valid = head + own + tail
    steps = jnp.maximum(lax.div(valid + (CHUNK - 1), CHUNK), 2)

    def panel_copy(i):
        rows = pl.ds(pl.multiple_of(i * CHUNK_ROWS, CHUNK_ROWS), CHUNK_ROWS)
        return pltpu.make_async_copy(panel.at[rows], panel_v.at[rows], panel_sem.at[i])

    shift = pl.multiple_of((lead + head - prev) * BLOCK, BLOCK)
    modes_copy = pltpu.make_async_copy(
        modes, modes_v.at[pl.ds(shift, modes.shape[0])], modes_sem
    )
    for i in range(2):
        panel_copy(i).start()
    modes_copy.start()

    def launch(i, carry):
        panel_copy(i).start()
        return carry

    lax.fori_loop(2, steps, launch, 0)
    gram[...] = jnp.zeros_like(gram)
    cross[...] = jnp.zeros_like(cross)

    def step(i, carry):
        first = i * CHUNK_ROWS
        panel_copy(i).wait()

        @pl.when(i == 0)
        def _():
            modes_copy.wait()

        rows = pl.ds(pl.multiple_of(first, CHUNK_ROWS), CHUNK_ROWS)
        values = panel_v[rows, :]
        gram[...] += transposed_product(kept_rows(values, first, 0, valid * BLOCK), values)
        beside = pl.ds(pl.multiple_of(first + lead * BLOCK, CHUNK_ROWS), CHUNK_ROWS)
        mode_values = kept_rows(modes_v[beside, :], first, head * BLOCK, (head + own) * BLOCK)
        cross[...] += transposed_product(mode_values, values)
        return carry

    lax.fori_loop(0, steps, step, 0)
    for i in range(2):
        for j in range(2):
            start = (2 * i + j) * LANES
            out[start : start + LANES, :] = gram[i * LANES : (i + 1) * LANES, j * LANES : (j + 1) * LANES]
        out[(4 + i) * LANES : (5 + i) * LANES, :] = cross[:, i * LANES : (i + 1) * LANES]


def edge_rows_kernel(
    moves, panel, from_prev, from_next, before, out, head_v, tail_v, prev_v, next_v, cross, sems
):
    head, tail, prev, following = moves[0], moves[1], moves[2], moves[3]
    edge_rows = from_prev.shape[0]
    lead = edge_rows // BLOCK
    own = 2 * lead - prev - following
    tail_start = pl.multiple_of((head + own) * BLOCK, BLOCK)
    shift = pl.multiple_of(head * BLOCK, BLOCK)
    copies = [
        pltpu.make_async_copy(panel.at[pl.ds(0, edge_rows)], head_v, sems.at[0]),
        pltpu.make_async_copy(from_prev, prev_v.at[pl.ds(shift, edge_rows)], sems.at[1]),
        pltpu.make_async_copy(panel.at[pl.ds(tail_start, edge_rows)], tail_v, sems.at[2]),
        pltpu.make_async_copy(from_next, next_v, sems.at[3]),
    ]
    for copy in copies:
        copy.start()
    cross[...] = jnp.zeros_like(cross)
    for copy in copies:
        copy.wait()

    def head_step(i, carry):
        first = i * CHUNK_ROWS
        rows = pl.ds(pl.multiple_of(first, CHUNK_ROWS), CHUNK_ROWS)
        beside = pl.ds(pl.multiple_of(first + edge_rows, CHUNK_ROWS), CHUNK_ROWS)
        mode_values = kept_rows(prev_v[beside, :], first, 0, head * BLOCK)
        cross[...] += transposed_product(mode_values, head_v[rows, :])
        return carry

    def tail_step(i, carry):
        first = i * CHUNK_ROWS
        rows = pl.ds(pl.multiple_of(first, CHUNK_ROWS), CHUNK_ROWS)
        mode_values = kept_rows(next_v[rows, :], first, 0, tail * BLOCK)
        cross[...] += transposed_product(mode_values, tail_v[rows, :])
        return carry

    lax.fori_loop(0, lax.div(head + (CHUNK - 1), CHUNK), head_step, 0)
    lax.fori_loop(0, lax.div(tail + (CHUNK - 1), CHUNK), tail_step, 0)
    out[: 4 * LANES, :] = before[: 4 * LANES, :]
    for i in range(2):
        rows = slice((4 + i) * LANES, (5 + i) * LANES)
        out[rows, :] = before[rows, :] + cross[:, i * LANES : (i + 1) * LANES]


def own_rows(moves, panel, modes):
    slots = panel.shape[0] // BLOCK
    spare = modes.shape[0] // 2
    return pl.pallas_call(
        own_rows_kernel,
        out_shape=jax.ShapeDtypeStruct((STACK, LANES), jnp.float32),
        in_specs=[
            pl.BlockSpec(memory_space=pltpu.SMEM),
            pl.BlockSpec(memory_space=pl.ANY),
            pl.BlockSpec(memory_space=pl.ANY),
        ],
        out_specs=pl.BlockSpec(memory_space=pltpu.VMEM),
        scratch_shapes=[
            pltpu.VMEM(panel.shape, panel.dtype),
            pltpu.VMEM((panel.shape[0] + spare, MODES), modes.dtype),
            pltpu.VMEM((MEMBERS, MEMBERS), jnp.float32),
            pltpu.VMEM((MODES, MEMBERS), jnp.float32),
            pltpu.SemaphoreType.DMA((slots // CHUNK,)),
            pltpu.SemaphoreType.DMA,
        ],
        compiler_params=pltpu.CompilerParams(vmem_limit_bytes=32 * 1024 * 1024),
        cost_estimate=pl.CostEstimate(
            flops=2 * 12288 * 384 * 256, bytes_accessed=10 * 1024 * 1024, transcendentals=0
        ),
        name="own_rows",
    )(moves, panel, modes)


def edge_rows(moves, panel, from_prev, from_next, before):
    rows = from_prev.shape[0]
    return pl.pallas_call(
        edge_rows_kernel,
        out_shape=jax.ShapeDtypeStruct((STACK, LANES), jnp.float32),
        in_specs=[
            pl.BlockSpec(memory_space=pltpu.SMEM),
            pl.BlockSpec(memory_space=pl.ANY),
            pl.BlockSpec(memory_space=pl.ANY),
            pl.BlockSpec(memory_space=pl.ANY),
            pl.BlockSpec(memory_space=pltpu.VMEM),
        ],
        out_specs=pl.BlockSpec(memory_space=pltpu.VMEM),
        scratch_shapes=[
            pltpu.VMEM((rows, MEMBERS), panel.dtype),
            pltpu.VMEM((rows, MEMBERS), panel.dtype),
            pltpu.VMEM((2 * rows, MODES), from_prev.dtype),
            pltpu.VMEM((rows, MODES), from_prev.dtype),
            pltpu.VMEM((MODES, MEMBERS), jnp.float32),
            pltpu.SemaphoreType.DMA((4,)),
        ],
        compiler_params=pltpu.CompilerParams(vmem_limit_bytes=32 * 1024 * 1024),
        cost_estimate=pl.CostEstimate(
            flops=2 * 4096 * 128 * 256, bytes_accessed=6 * 1024 * 1024, transcendentals=0
        ),
        name="edge_rows",
    )(moves, panel, from_prev, from_next, before)


def projected(product, inverse_t):
    high = product.astype(jnp.bfloat16)
    rest = product - high.astype(jnp.float32)
    middle = rest.astype(jnp.bfloat16)
    low = (rest - middle.astype(jnp.float32)).astype(jnp.bfloat16)

    def part(values):
        return lax.dot_general(
            values, inverse_t, (((1,), (1,)), ((), ())), preferred_element_type=jnp.float32
        )

    return part(low) + part(middle) + part(high)


def factor_kernel(core, mine, other, factor, projection, work, packed, cross):
    half = mine.shape[0]

    def place(lower, upper):
        for index in range(2 * half // LANES):
            source = lower if index * LANES < half else upper
            start = index * LANES % half
            square = source[start : start + LANES, :]
            columns = slice(index % 2 * LANES, (index % 2 + 1) * LANES)
            if index < 4:
                work[index // 2 * LANES : (index // 2 + 1) * LANES, columns] = square
            else:
                cross[:, columns] = square

    @pl.when(core[0] == 0)
    def _():
        place(mine, other)

    @pl.when(core[0] != 0)
    def _():
        place(other, mine)

    size = MEMBERS
    lanes = lax.broadcasted_iota(jnp.int32, (TILE, size), 1)
    subs = lax.broadcasted_iota(jnp.int32, (TILE, size), 0)
    near = lax.broadcasted_iota(jnp.int32, (TILE, LANES), 0)
    groups = size // TILE

    def wide(values):
        return jnp.concatenate([values, values], axis=1)

    for group in range(groups):
        base = group * TILE
        panel = work[base : base + TILE, :]
        columns = [
            jnp.broadcast_to(panel[:, base + r : base + r + 1], (TILE, LANES)) for r in range(TILE)
        ]
        for r in range(TILE):
            column = columns[r]
            pivot = jnp.broadcast_to(column[r : r + 1, :], (TILE, LANES))
            recip = 1.0 / pivot
            scale = lax.rsqrt(pivot)
            panel = jnp.where(lanes == base + r, jnp.where(subs == r, 1.0, 0.0), panel)
            row = jnp.broadcast_to(panel[r : r + 1, :], (TILE, size))
            packed[base + r : base + r + 1, :] = (row * wide(scale))[0:1]
            solved = row * wide(recip)
            panel = jnp.where(subs == r, solved, panel - wide(column) * solved)
            for s in range(r + 1, TILE):
                entry = jnp.broadcast_to(columns[s][r : r + 1, :], (TILE, LANES)) * recip
                columns[s] = jnp.where(near == r, entry, columns[s] - column * entry)
        inside = (lanes >= base) & (lanes < base + TILE)
        solved_rows = [jnp.broadcast_to(panel[q : q + 1, :], (TILE, size)) for q in range(TILE)]
        for i in range(group + 1, groups):
            rows = slice(i * TILE, (i + 1) * TILE)
            old = work[rows, :]
            fresh = jnp.where(inside, 0.0, old)
            for q in range(TILE):
                coefficient = jnp.broadcast_to(old[:, base + q : base + q + 1], (TILE, size))
                fresh = fresh - coefficient * solved_rows[q]
            work[rows, :] = fresh

    row = lax.broadcasted_iota(jnp.int32, (size, size), 0)
    column = lax.broadcasted_iota(jnp.int32, (size, size), 1)
    result = packed[...]
    factor[...] = jnp.where(
        column > row, result, jnp.where(column == row, 1.0 / result, jnp.zeros_like(result))
    )
    inverse_t = jnp.where(column <= row, result, jnp.zeros_like(result)).astype(jnp.bfloat16)
    projection[...] = projected(cross[...], inverse_t)


def factor_and_projection(core, mine, other):
    vmem = pl.BlockSpec(memory_space=pltpu.VMEM)
    return pl.pallas_call(
        factor_kernel,
        out_shape=(
            jax.ShapeDtypeStruct((MEMBERS, MEMBERS), jnp.float32),
            jax.ShapeDtypeStruct((MODES, MEMBERS), jnp.float32),
        ),
        in_specs=[pl.BlockSpec(memory_space=pltpu.SMEM), vmem, vmem],
        out_specs=(vmem, vmem),
        scratch_shapes=[
            pltpu.VMEM((MEMBERS, MEMBERS), jnp.float32),
            pltpu.VMEM((MEMBERS, MEMBERS), jnp.float32),
            pltpu.VMEM((MODES, MEMBERS), jnp.float32),
        ],
        name="factor_and_projection",
    )(core, mine, other)


def to_all(values, axes):
    count = lax.axis_size(axes)
    copies = jnp.broadcast_to(values[None], (count,) + values.shape)
    return lax.all_to_all(copies, axes, 0, 0)


def swapped(values):
    return lax.ppermute(values, "c", [(0, 1), (1, 0)])


def summed_half(stack):
    core = lax.axis_index("c")
    half = stack.shape[0] // 2
    keep = lax.dynamic_slice_in_dim(stack, core * half, half, 0)
    give = lax.dynamic_slice_in_dim(stack, (1 - core) * half, half, 0)
    share = keep + swapped(give)
    count = lax.axis_size(("y", "g"))
    pieces = share.reshape(count, half // count, LANES)
    piece = lax.all_to_all(pieces, ("y", "g"), 0, 0).sum(0)
    piece = to_all(piece, "z").sum(0)
    return to_all(piece, ("y", "g")).reshape(half, LANES)


def body(sensitivity, block_moves, shape_modes):
    panel = sensitivity[0]
    modes = shape_modes[0]
    moves = block_moves[0, 0]
    edge = modes.shape[0] // 2
    chain = ("y", "z", "c")
    count = lax.axis_size(chain)
    from_next = lax.ppermute(modes[:edge], chain, [(i + 1, i) for i in range(count - 1)])
    from_prev = lax.ppermute(modes[edge:], chain, [(i, i + 1) for i in range(count - 1)])
    stack = own_rows(moves, panel, modes)
    stack = edge_rows(moves, panel, from_prev, from_next, stack)
    mine = summed_half(stack)
    other = swapped(mine)
    core = lax.axis_index("c").astype(jnp.int32).reshape(1)
    return factor_and_projection(core, mine, other)


def solution(mesh):
    split = Mesh(mesh.devices.reshape(4, 8, 2, 4), ("y", "z", "c", "g"))
    spec = P("g", ("y", "z", "c"), None)
    return jax.shard_map(
        body, mesh=split, in_specs=(spec, spec, spec), out_specs=(P(), P()), check_vma=False
    )
```

```python
import functools

import jax
import jax.numpy as jnp
from jax import lax
from jax.experimental import pallas as pl
from jax.experimental.pallas import tpu as pltpu
from jax.sharding import Mesh, PartitionSpec as P

BLOCK = 128
LANES = 128
MEMBERS = 256
MODES = 128
BLOCKS = 64
CHUNK = 16
CHUNK_ROWS = CHUNK * BLOCK
TILE = 8
STACK = 640
NEAR = 21
FAR = 11
NEAR_ROWS = NEAR * BLOCK
FAR_ROWS = FAR * BLOCK
PARCEL = 2 * FAR_ROWS
VMEM_BYTES = 51 * 1024 * 1024
EDGE_VMEM_BYTES = 45 * 1024 * 1024


def transposed_product(a, b):
    return lax.dot_general(a, b, (((0,), (0,)), ((), ())), preferred_element_type=jnp.float32)


def kept_blocks(values, first, start, stop):
    parts = []
    for index in range(values.shape[0] // BLOCK):
        part = values[index * BLOCK : (index + 1) * BLOCK, :]
        keep = (first + index >= start) & (first + index < stop)
        parts.append(jnp.where(keep, part, jnp.zeros_like(part)))
    return jnp.concatenate(parts, axis=0)


def block_rows(start, count):
    return pl.ds(pl.multiple_of(start * BLOCK, BLOCK), count * BLOCK)


def parcels_kernel(core, moves, panel, modes, to_inner, to_outer, sems):
    head, tail, prev, following = moves[0], moves[1], moves[2], moves[3]
    block_total = modes.shape[0] // BLOCK
    tail_start = head + block_total - prev - following
    second = core[0] != 0

    def far_copies(start, out, which):
        return [
            pltpu.make_async_copy(
                panel.at[block_rows(start, FAR), pl.ds(half * LANES, LANES)],
                out.at[pl.ds(half * FAR_ROWS, FAR_ROWS)],
                sems.at[which, half],
            )
            for half in range(2)
        ]

    def near_copies(start, out, which):
        return [
            pltpu.make_async_copy(
                modes.at[pl.ds(start * BLOCK, NEAR_ROWS)],
                out.at[pl.ds(0, NEAR_ROWS)],
                sems.at[which, 0],
            )
        ]

    choices = []
    for here, to_prev, to_next in (
        (second, to_inner, to_outer),
        (jnp.logical_not(second), to_outer, to_inner),
    ):
        choices += [
            (here & (head > 0), far_copies(0, to_prev, 0)),
            (here & (head == 0), near_copies(0, to_prev, 0)),
            (here & (tail > 0), far_copies(tail_start + NEAR, to_next, 1)),
            (here & (tail == 0), near_copies(block_total - NEAR, to_next, 1)),
        ]
    for chosen, copies in choices:

        @pl.when(chosen)
        def _():
            for copy in copies:
                copy.start()

    for chosen, copies in choices:

        @pl.when(chosen)
        def _():
            for copy in copies:
                copy.wait()


def own_rows_kernel(
    moves, panel, modes, out, panel_v, modes_v, gram, cross, panel_sem, modes_sem
):
    head, tail, prev, following = moves[0], moves[1], moves[2], moves[3]
    block_total = modes.shape[0] // BLOCK
    lead = block_total // 2
    own = block_total - prev - following
    valid = head + own + tail
    steps = jnp.maximum(lax.div(valid + (CHUNK - 1), CHUNK), 1)

    def panel_copy(i):
        rows = block_rows(i * CHUNK, CHUNK)
        return pltpu.make_async_copy(panel.at[rows], panel_v.at[rows], panel_sem.at[i])

    modes_copy = pltpu.make_async_copy(
        modes, modes_v.at[block_rows(lead + head - prev, block_total)], modes_sem
    )
    panel_copy(0).start()
    modes_copy.start()

    def launch(i, carry):
        panel_copy(i).start()
        return carry

    lax.fori_loop(1, steps, launch, 0)
    gram[...] = jnp.zeros_like(gram)
    cross[...] = jnp.zeros_like(cross)
    modes_copy.wait()

    def step(i, carry):
        panel_copy(i).wait()
        block = i * CHUNK
        values = panel_v[block_rows(block, CHUNK), :]
        beside = modes_v[block_rows(block + lead, CHUNK), :]
        gram[...] += transposed_product(values, kept_blocks(values, block, 0, valid))
        cross[...] += transposed_product(kept_blocks(beside, block, head, head + own), values)
        return carry

    lax.fori_loop(0, steps, step, 0)
    out[:LANES, :] = gram[:LANES, :LANES]
    out[LANES : 2 * LANES, :] = gram[:LANES, LANES:]
    out[2 * LANES : 3 * LANES, :] = gram[LANES:, LANES:]
    for i in range(2):
        out[(3 + i) * LANES : (4 + i) * LANES, :] = cross[:, i * LANES : (i + 1) * LANES]


class Edge:
    def __init__(self, from_prev, moves, block_total):
        head, tail, prev, following = moves[0], moves[1], moves[2], moves[3]
        own = block_total - prev - following
        far_start = jnp.minimum(block_total - following, block_total - FAR)
        self.near = jnp.where(from_prev, head, tail)
        self.near_source = jnp.where(from_prev, jnp.maximum(head - NEAR, 0), head + own)
        self.near_offset = jnp.where(from_prev, jnp.minimum(head, NEAR), NEAR)
        self.near_first = jnp.where(from_prev, NEAR - head, 0)
        self.near_stop = jnp.where(from_prev, NEAR, tail)
        self.far = jnp.where(from_prev, prev, following) - NEAR
        self.far_source = jnp.where(from_prev, NEAR, far_start)

    def copies(self, panel, modes, near_v, far_v, sems):
        near = pltpu.make_async_copy(
            panel.at[block_rows(self.near_source, NEAR)],
            near_v.at[pl.ds(NEAR_ROWS, NEAR_ROWS)],
            sems.at[0],
        )
        far = pltpu.make_async_copy(
            modes.at[block_rows(self.far_source, FAR)], far_v, sems.at[1]
        )
        return [(self.near > 0, near), (self.far > 0, far)]

    def multiply(self, near_v, far_v, parcel, out):
        def add(index, values):
            out[index * LANES : (index + 1) * LANES, :] += values

        @pl.when(self.near > 0)
        def _():
            mode_values = kept_blocks(parcel[:NEAR_ROWS, :], 0, self.near_first, self.near_stop)
            panel_values = near_v[block_rows(self.near_offset, NEAR), :]
            product = transposed_product(mode_values, panel_values)
            for i in range(2):
                add(3 + i, product[:, i * LANES : (i + 1) * LANES])

        @pl.when(self.far > 0)
        def _():
            mode_values = kept_blocks(far_v[...], 0, 0, self.far)
            for i in range(2):
                values = parcel[i * FAR_ROWS : (i + 1) * FAR_ROWS, :]
                add(3 + i, transposed_product(mode_values, values))


def inner_edge_kernel(
    core, moves, panel, modes, parcel, before, out, outer_near, outer_far, near_v, far_v, sems
):
    block_total = modes.shape[0] // BLOCK
    inner = Edge(core[0] != 0, moves, block_total)
    outer = Edge(core[0] == 0, moves, block_total)
    inner_copies = inner.copies(panel, modes, near_v, far_v, sems.at[0])
    outer_copies = outer.copies(panel, modes, outer_near, outer_far, sems.at[1])
    for needed, copy in inner_copies + outer_copies:
        pl.when(needed)(copy.start)
    filler = jnp.zeros((NEAR_ROWS, MEMBERS), near_v.dtype)
    near_v[:NEAR_ROWS, :] = filler
    outer_near[:NEAR_ROWS, :] = filler
    out[...] = before[...]
    for needed, copy in inner_copies:
        pl.when(needed)(copy.wait)
    inner.multiply(near_v, far_v, parcel, out)
    for needed, copy in outer_copies:
        pl.when(needed)(copy.wait)


def outer_edge_kernel(core, moves, outer_near, outer_far, parcel, before, out):
    outer = Edge(core[0] == 0, moves, BLOCKS)
    out[...] = before[...]
    outer.multiply(outer_near, outer_far, parcel, out)


SMEM = pl.BlockSpec(memory_space=pltpu.SMEM)
VMEM = pl.BlockSpec(memory_space=pltpu.VMEM)
HBM = pl.BlockSpec(memory_space=pltpu.HBM)


def parcels(core, moves, panel, modes):
    parcel = jax.ShapeDtypeStruct((PARCEL, LANES), modes.dtype)
    return pl.pallas_call(
        parcels_kernel,
        out_shape=(parcel, parcel),
        in_specs=[SMEM, SMEM, HBM, HBM],
        out_specs=(VMEM, VMEM),
        scratch_shapes=[pltpu.SemaphoreType.DMA((2, 2))],
        compiler_params=pltpu.CompilerParams(vmem_limit_bytes=VMEM_BYTES),
        cost_estimate=pl.CostEstimate(flops=0, bytes_accessed=3 * 1024 * 1024, transcendentals=0),
        name="parcels",
    )(core, moves, panel, modes)


def own_rows(moves, panel, modes):
    slots = panel.shape[0] // BLOCK
    return pl.pallas_call(
        own_rows_kernel,
        out_shape=jax.ShapeDtypeStruct((STACK, LANES), jnp.float32),
        in_specs=[SMEM, HBM, HBM],
        out_specs=VMEM,
        scratch_shapes=[
            pltpu.VMEM(panel.shape, panel.dtype),
            pltpu.VMEM((panel.shape[0] + modes.shape[0] // 2, MODES), modes.dtype),
            pltpu.VMEM((MEMBERS, MEMBERS), jnp.float32),
            pltpu.VMEM((MODES, MEMBERS), jnp.float32),
            pltpu.SemaphoreType.DMA((slots // CHUNK,)),
            pltpu.SemaphoreType.DMA,
        ],
        compiler_params=pltpu.CompilerParams(vmem_limit_bytes=VMEM_BYTES),
        cost_estimate=pl.CostEstimate(
            flops=2 * 12288 * 384 * 256, bytes_accessed=10 * 1024 * 1024, transcendentals=0
        ),
        name="own_rows",
    )(moves, panel, modes)


def inner_edge(core, moves, panel, modes, parcel, before):
    near = (2 * NEAR_ROWS, MEMBERS)
    far = (FAR_ROWS, MODES)
    return pl.pallas_call(
        inner_edge_kernel,
        out_shape=(
            jax.ShapeDtypeStruct((STACK, LANES), jnp.float32),
            jax.ShapeDtypeStruct(near, panel.dtype),
            jax.ShapeDtypeStruct(far, modes.dtype),
        ),
        in_specs=[SMEM, SMEM, HBM, HBM, VMEM, VMEM],
        out_specs=(VMEM, VMEM, VMEM),
        scratch_shapes=[
            pltpu.VMEM(near, panel.dtype),
            pltpu.VMEM(far, modes.dtype),
            pltpu.SemaphoreType.DMA((2, 2)),
        ],
        compiler_params=pltpu.CompilerParams(vmem_limit_bytes=EDGE_VMEM_BYTES),
        cost_estimate=pl.CostEstimate(
            flops=2 * 2048 * 128 * 256, bytes_accessed=4 * 1024 * 1024, transcendentals=0
        ),
        name="inner_edge",
    )(core, moves, panel, modes, parcel, before)


def outer_edge(core, moves, near, far, parcel, before):
    return pl.pallas_call(
        outer_edge_kernel,
        out_shape=jax.ShapeDtypeStruct((STACK, LANES), jnp.float32),
        in_specs=[SMEM, SMEM, VMEM, VMEM, VMEM, VMEM],
        out_specs=VMEM,
        compiler_params=pltpu.CompilerParams(vmem_limit_bytes=EDGE_VMEM_BYTES),
        cost_estimate=pl.CostEstimate(
            flops=2 * 2048 * 128 * 256, bytes_accessed=2 * 1024 * 1024, transcendentals=0
        ),
        name="outer_edge",
    )(core, moves, near, far, parcel, before)


def projected(product, inverse_t):
    high = product.astype(jnp.bfloat16)
    rest = product - high.astype(jnp.float32)
    middle = rest.astype(jnp.bfloat16)
    low = (rest - middle.astype(jnp.float32)).astype(jnp.bfloat16)

    def part(values):
        return lax.dot_general(
            values, inverse_t, (((1,), (1,)), ((), ())), preferred_element_type=jnp.float32
        )

    return part(low) + part(middle) + part(high)


def factor_kernel(stack, factor, projection, work, packed, cross):
    squares = [stack[i * LANES : (i + 1) * LANES, :] for i in range(STACK // LANES)]
    work[:LANES, :LANES] = squares[0]
    work[:LANES, LANES:] = squares[1]
    work[LANES:, :LANES] = squares[1].T
    work[LANES:, LANES:] = squares[2]
    cross[:, :LANES] = squares[3]
    cross[:, LANES:] = squares[4]

    size = MEMBERS
    lanes = lax.broadcasted_iota(jnp.int32, (TILE, LANES), 1)
    subs = lax.broadcasted_iota(jnp.int32, (TILE, LANES), 0)
    groups = size // TILE
    halves = size // LANES

    def row_of(values, r):
        return jnp.broadcast_to(values[r : r + 1, :], (TILE, LANES))

    def column_of(values, c):
        return jnp.broadcast_to(values[:, c : c + 1], (TILE, LANES))

    def loaded(i):
        return [work[i * TILE : (i + 1) * TILE, h * LANES : (h + 1) * LANES] for h in range(halves)]

    def reduced(old, before):
        half, start, solved_rows = before
        fresh = list(old)
        inside = (lanes >= start) & (lanes < start + TILE)
        fresh[half] = jnp.where(inside, 0.0, old[half])
        for q in range(TILE):
            coefficient = column_of(old[half], start + q)
            for h in range(halves):
                fresh[h] = fresh[h] - coefficient * solved_rows[q][h]
        return fresh

    def bf16_parts(values, order):
        parts = []
        for _ in range(3):
            part = values.astype(jnp.bfloat16).astype(jnp.float32)
            parts.append(part)
            values = values - part
        return jnp.concatenate([parts[k] for k in order], axis=0).astype(jnp.bfloat16)

    before = None
    for group in range(groups):
        half, start = divmod(group * TILE, LANES)
        panel = loaded(group)
        if before is not None:
            panel = reduced(panel, before)
        raw = list(panel)
        columns = [column_of(panel[half], start + r) for r in range(TILE)]
        below = list(range(group + 1, groups)) if before is not None else []
        for r in range(TILE):
            column = columns[r]
            at_row = subs == r
            at_lane = lanes == start + r
            recip = 1.0 / row_of(column, r)
            scale = lax.rsqrt(row_of(column, r))
            factor_of = jnp.where(at_row, -1.0, column)
            for s in range(r + 1, TILE):
                kept = jnp.where(at_row, 0.0, columns[s])
                columns[s] = kept - (factor_of * row_of(columns[s], r)) * recip
            index = group * TILE + r
            for h in range(halves):
                row = row_of(panel[h], r)
                kept = jnp.where(at_row, 0.0, panel[h])
                if h == half:
                    row = jnp.where(at_lane, 1.0, row)
                    kept = jnp.where(at_lane, 0.0, kept)
                packed[index : index + 1, h * LANES : (h + 1) * LANES] = (row * scale)[0:1]
                panel[h] = kept - (factor_of * row) * recip
            for i in below[r::TILE]:
                fresh = loaded(i)
                inside = (lanes >= before[1]) & (lanes < before[1] + TILE)
                fresh[before[0]] = jnp.where(inside, 0.0, fresh[before[0]])
                for h in range(halves):
                    part = update[i * TILE - first : (i + 1) * TILE - first, h * LANES : (h + 1) * LANES]
                    work[i * TILE : (i + 1) * TILE, h * LANES : (h + 1) * LANES] = fresh[h] - part
        before = (half, start, [[row_of(panel[h], q) for h in range(halves)] for q in range(TILE)])
        first = half * LANES
        left = bf16_parts(jnp.concatenate(raw[half:], axis=1), (0, 0, 0, 1, 1, 2))
        right = bf16_parts(jnp.concatenate(panel, axis=1), (0, 1, 2, 0, 1, 0))
        update = transposed_product(left, right)

    row = lax.broadcasted_iota(jnp.int32, (size, size), 0)
    column = lax.broadcasted_iota(jnp.int32, (size, size), 1)
    result = packed[...]
    factor[...] = jnp.where(
        column > row, result, jnp.where(column == row, 1.0 / result, jnp.zeros_like(result))
    )
    inverse_t = jnp.where(column <= row, result, jnp.zeros_like(result)).astype(jnp.bfloat16)
    projection[...] = projected(cross[...], inverse_t)


def factor_and_projection(stack):
    return pl.pallas_call(
        factor_kernel,
        out_shape=(
            jax.ShapeDtypeStruct((MEMBERS, MEMBERS), jnp.float32),
            jax.ShapeDtypeStruct((MODES, MEMBERS), jnp.float32),
        ),
        in_specs=[VMEM],
        out_specs=(VMEM, VMEM),
        scratch_shapes=[
            pltpu.VMEM((MEMBERS, MEMBERS), jnp.float32),
            pltpu.VMEM((MEMBERS, MEMBERS), jnp.float32),
            pltpu.VMEM((MODES, MEMBERS), jnp.float32),
        ],
        name="factor_and_projection",
    )(stack)


def to_all(values, axes):
    count = lax.axis_size(axes)
    copies = jnp.broadcast_to(values[None], (count,) + values.shape)
    return lax.all_to_all(copies, axes, 0, 0)


def summed(stack):
    axes = ("y", "g")
    count = lax.axis_size(axes)
    pieces = stack.reshape(count, stack.shape[0] // count, LANES)
    piece = lax.all_to_all(pieces, axes, 0, 0).sum(0)
    piece = piece + lax.ppermute(piece, "c", [(0, 1), (1, 0)])
    piece = to_all(piece, "z").sum(0)
    return to_all(piece, axes).reshape(stack.shape)


def body(sensitivity, block_moves, shape_modes):
    panel = sensitivity[0]
    modes = shape_modes[0]
    moves = block_moves[0, 0]
    core = lax.axis_index("c").astype(jnp.int32).reshape(1)
    chain = ("y", "z", "c")
    count = lax.axis_size(chain)
    to_inner, to_outer = parcels(core, moves, panel, modes)
    pairs = range(1, count - 1, 2)
    outer = lax.ppermute(
        to_outer, chain, [(i, i + 1) for i in pairs] + [(i + 1, i) for i in pairs]
    )
    inner = lax.ppermute(to_inner, chain, [(i, i ^ 1) for i in range(count)])
    stack = own_rows(moves, panel, modes)
    stack, near, far = inner_edge(core, moves, panel, modes, inner, stack)
    stack = outer_edge(core, moves, near, far, outer, stack)
    return factor_and_projection(summed(stack))


def solution(mesh):
    split = Mesh(mesh.devices.reshape(4, 8, 2, 4), ("y", "z", "c", "g"))
    spec = P("g", ("y", "z", "c"), None)
    return jax.shard_map(
        body, mesh=split, in_specs=(spec, spec, spec), out_specs=(P(), P()), check_vma=False
    )
```

```python
import functools

import jax
import jax.numpy as jnp
from jax import lax
from jax.experimental import pallas as pl
from jax.experimental.pallas import tpu as pltpu
from jax.sharding import Mesh, PartitionSpec as P

BLOCK = 128
LANES = 128
MEMBERS = 256
MODES = 128
BLOCKS = 64
CHUNK = 16
CHUNK_ROWS = CHUNK * BLOCK
SUBLANES = 8
TILE = 16
STACK = 640
NEAR = 21
FAR = 11
NEAR_ROWS = NEAR * BLOCK
FAR_ROWS = FAR * BLOCK
PARCEL = 2 * FAR_ROWS
VMEM_BYTES = 51 * 1024 * 1024
EDGE_VMEM_BYTES = 45 * 1024 * 1024


def transposed_product(a, b):
    return lax.dot_general(a, b, (((0,), (0,)), ((), ())), preferred_element_type=jnp.float32)


def kept_blocks(values, first, start, stop):
    parts = []
    for index in range(values.shape[0] // BLOCK):
        part = values[index * BLOCK : (index + 1) * BLOCK, :]
        keep = (first + index >= start) & (first + index < stop)
        parts.append(jnp.where(keep, part, jnp.zeros_like(part)))
    return jnp.concatenate(parts, axis=0)


def block_rows(start, count):
    return pl.ds(pl.multiple_of(start * BLOCK, BLOCK), count * BLOCK)


def parcels_kernel(core, moves, panel, modes, to_inner, to_outer, sems):
    head, tail, prev, following = moves[0], moves[1], moves[2], moves[3]
    block_total = modes.shape[0] // BLOCK
    tail_start = head + block_total - prev - following
    second = core[0] != 0

    def far_copies(start, out, which):
        return [
            pltpu.make_async_copy(
                panel.at[block_rows(start, FAR), pl.ds(half * LANES, LANES)],
                out.at[pl.ds(half * FAR_ROWS, FAR_ROWS)],
                sems.at[which, half],
            )
            for half in range(2)
        ]

    def near_copies(start, out, which):
        return [
            pltpu.make_async_copy(
                modes.at[pl.ds(start * BLOCK, NEAR_ROWS)],
                out.at[pl.ds(0, NEAR_ROWS)],
                sems.at[which, 0],
            )
        ]

    choices = []
    for here, to_prev, to_next in (
        (second, to_inner, to_outer),
        (jnp.logical_not(second), to_outer, to_inner),
    ):
        choices += [
            (here & (head > 0), far_copies(0, to_prev, 0)),
            (here & (head == 0), near_copies(0, to_prev, 0)),
            (here & (tail > 0), far_copies(tail_start + NEAR, to_next, 1)),
            (here & (tail == 0), near_copies(block_total - NEAR, to_next, 1)),
        ]
    for chosen, copies in choices:

        @pl.when(chosen)
        def _():
            for copy in copies:
                copy.start()

    for chosen, copies in choices:

        @pl.when(chosen)
        def _():
            for copy in copies:
                copy.wait()


def own_rows_kernel(
    moves, panel, modes, out, panel_v, modes_v, gram, cross, panel_sem, modes_sem
):
    head, tail, prev, following = moves[0], moves[1], moves[2], moves[3]
    block_total = modes.shape[0] // BLOCK
    lead = block_total // 2
    own = block_total - prev - following
    valid = head + own + tail
    steps = jnp.maximum(lax.div(valid + (CHUNK - 1), CHUNK), 1)

    def panel_copy(i):
        rows = block_rows(i * CHUNK, CHUNK)
        return pltpu.make_async_copy(panel.at[rows], panel_v.at[rows], panel_sem.at[i])

    modes_copy = pltpu.make_async_copy(
        modes, modes_v.at[block_rows(lead + head - prev, block_total)], modes_sem
    )
    panel_copy(0).start()
    modes_copy.start()

    def launch(i, carry):
        panel_copy(i).start()
        return carry

    lax.fori_loop(1, steps, launch, 0)
    gram[...] = jnp.zeros_like(gram)
    cross[...] = jnp.zeros_like(cross)
    modes_copy.wait()

    def step(i, carry):
        panel_copy(i).wait()
        block = i * CHUNK
        values = panel_v[block_rows(block, CHUNK), :]
        beside = modes_v[block_rows(block + lead, CHUNK), :]
        gram[...] += transposed_product(values, kept_blocks(values, block, 0, valid))
        cross[...] += transposed_product(kept_blocks(beside, block, head, head + own), values)
        return carry

    lax.fori_loop(0, steps, step, 0)
    out[:LANES, :] = gram[:LANES, :LANES]
    out[LANES : 2 * LANES, :] = gram[:LANES, LANES:]
    out[2 * LANES : 3 * LANES, :] = gram[LANES:, LANES:]
    for i in range(2):
        out[(3 + i) * LANES : (4 + i) * LANES, :] = cross[:, i * LANES : (i + 1) * LANES]


class Edge:
    def __init__(self, from_prev, moves, block_total):
        head, tail, prev, following = moves[0], moves[1], moves[2], moves[3]
        own = block_total - prev - following
        far_start = jnp.minimum(block_total - following, block_total - FAR)
        self.near = jnp.where(from_prev, head, tail)
        self.near_source = jnp.where(from_prev, jnp.maximum(head - NEAR, 0), head + own)
        self.near_offset = jnp.where(from_prev, jnp.minimum(head, NEAR), NEAR)
        self.near_first = jnp.where(from_prev, NEAR - head, 0)
        self.near_stop = jnp.where(from_prev, NEAR, tail)
        self.far = jnp.where(from_prev, prev, following) - NEAR
        self.far_source = jnp.where(from_prev, NEAR, far_start)

    def copies(self, panel, modes, near_v, far_v, sems):
        near = pltpu.make_async_copy(
            panel.at[block_rows(self.near_source, NEAR)],
            near_v.at[pl.ds(NEAR_ROWS, NEAR_ROWS)],
            sems.at[0],
        )
        far = pltpu.make_async_copy(
            modes.at[block_rows(self.far_source, FAR)], far_v, sems.at[1]
        )
        return [(self.near > 0, near), (self.far > 0, far)]

    def multiply(self, near_v, far_v, parcel, out):
        def add(index, values):
            out[index * LANES : (index + 1) * LANES, :] += values

        @pl.when(self.near > 0)
        def _():
            mode_values = kept_blocks(parcel[:NEAR_ROWS, :], 0, self.near_first, self.near_stop)
            panel_values = near_v[block_rows(self.near_offset, NEAR), :]
            product = transposed_product(mode_values, panel_values)
            for i in range(2):
                add(3 + i, product[:, i * LANES : (i + 1) * LANES])

        @pl.when(self.far > 0)
        def _():
            mode_values = kept_blocks(far_v[...], 0, 0, self.far)
            for i in range(2):
                values = parcel[i * FAR_ROWS : (i + 1) * FAR_ROWS, :]
                add(3 + i, transposed_product(mode_values, values))


def inner_edge_kernel(
    core, moves, panel, modes, parcel, before, out, outer_near, outer_far, near_v, far_v, sems
):
    block_total = modes.shape[0] // BLOCK
    inner = Edge(core[0] != 0, moves, block_total)
    outer = Edge(core[0] == 0, moves, block_total)
    inner_copies = inner.copies(panel, modes, near_v, far_v, sems.at[0])
    outer_copies = outer.copies(panel, modes, outer_near, outer_far, sems.at[1])
    for needed, copy in inner_copies + outer_copies:
        pl.when(needed)(copy.start)
    filler = jnp.zeros((NEAR_ROWS, MEMBERS), near_v.dtype)
    near_v[:NEAR_ROWS, :] = filler
    outer_near[:NEAR_ROWS, :] = filler
    out[...] = before[...]
    for needed, copy in inner_copies:
        pl.when(needed)(copy.wait)
    inner.multiply(near_v, far_v, parcel, out)
    for needed, copy in outer_copies:
        pl.when(needed)(copy.wait)


def outer_edge_kernel(core, moves, outer_near, outer_far, parcel, before, out):
    outer = Edge(core[0] == 0, moves, BLOCKS)
    out[...] = before[...]
    outer.multiply(outer_near, outer_far, parcel, out)


SMEM = pl.BlockSpec(memory_space=pltpu.SMEM)
VMEM = pl.BlockSpec(memory_space=pltpu.VMEM)
HBM = pl.BlockSpec(memory_space=pltpu.HBM)


def parcels(core, moves, panel, modes):
    parcel = jax.ShapeDtypeStruct((PARCEL, LANES), modes.dtype)
    return pl.pallas_call(
        parcels_kernel,
        out_shape=(parcel, parcel),
        in_specs=[SMEM, SMEM, HBM, HBM],
        out_specs=(VMEM, VMEM),
        scratch_shapes=[pltpu.SemaphoreType.DMA((2, 2))],
        compiler_params=pltpu.CompilerParams(vmem_limit_bytes=VMEM_BYTES),
        cost_estimate=pl.CostEstimate(flops=0, bytes_accessed=3 * 1024 * 1024, transcendentals=0),
        name="parcels",
    )(core, moves, panel, modes)


def own_rows(moves, panel, modes):
    slots = panel.shape[0] // BLOCK
    return pl.pallas_call(
        own_rows_kernel,
        out_shape=jax.ShapeDtypeStruct((STACK, LANES), jnp.float32),
        in_specs=[SMEM, HBM, HBM],
        out_specs=VMEM,
        scratch_shapes=[
            pltpu.VMEM(panel.shape, panel.dtype),
            pltpu.VMEM((panel.shape[0] + modes.shape[0] // 2, MODES), modes.dtype),
            pltpu.VMEM((MEMBERS, MEMBERS), jnp.float32),
            pltpu.VMEM((MODES, MEMBERS), jnp.float32),
            pltpu.SemaphoreType.DMA((slots // CHUNK,)),
            pltpu.SemaphoreType.DMA,
        ],
        compiler_params=pltpu.CompilerParams(vmem_limit_bytes=VMEM_BYTES),
        cost_estimate=pl.CostEstimate(
            flops=2 * 12288 * 384 * 256, bytes_accessed=10 * 1024 * 1024, transcendentals=0
        ),
        name="own_rows",
    )(moves, panel, modes)


def inner_edge(core, moves, panel, modes, parcel, before):
    near = (2 * NEAR_ROWS, MEMBERS)
    far = (FAR_ROWS, MODES)
    return pl.pallas_call(
        inner_edge_kernel,
        out_shape=(
            jax.ShapeDtypeStruct((STACK, LANES), jnp.float32),
            jax.ShapeDtypeStruct(near, panel.dtype),
            jax.ShapeDtypeStruct(far, modes.dtype),
        ),
        in_specs=[SMEM, SMEM, HBM, HBM, VMEM, VMEM],
        out_specs=(VMEM, VMEM, VMEM),
        scratch_shapes=[
            pltpu.VMEM(near, panel.dtype),
            pltpu.VMEM(far, modes.dtype),
            pltpu.SemaphoreType.DMA((2, 2)),
        ],
        compiler_params=pltpu.CompilerParams(vmem_limit_bytes=EDGE_VMEM_BYTES),
        cost_estimate=pl.CostEstimate(
            flops=2 * 2048 * 128 * 256, bytes_accessed=4 * 1024 * 1024, transcendentals=0
        ),
        name="inner_edge",
    )(core, moves, panel, modes, parcel, before)


def outer_edge(core, moves, near, far, parcel, before):
    return pl.pallas_call(
        outer_edge_kernel,
        out_shape=jax.ShapeDtypeStruct((STACK, LANES), jnp.float32),
        in_specs=[SMEM, SMEM, VMEM, VMEM, VMEM, VMEM],
        out_specs=VMEM,
        compiler_params=pltpu.CompilerParams(vmem_limit_bytes=EDGE_VMEM_BYTES),
        cost_estimate=pl.CostEstimate(
            flops=2 * 2048 * 128 * 256, bytes_accessed=2 * 1024 * 1024, transcendentals=0
        ),
        name="outer_edge",
    )(core, moves, near, far, parcel, before)


def projected(product, inverse_t):
    high = product.astype(jnp.bfloat16)
    rest = product - high.astype(jnp.float32)
    middle = rest.astype(jnp.bfloat16)
    low = (rest - middle.astype(jnp.float32)).astype(jnp.bfloat16)

    def part(values):
        return lax.dot_general(
            values, inverse_t, (((1,), (1,)), ((), ())), preferred_element_type=jnp.float32
        )

    return part(low) + part(middle) + part(high)


def factor_kernel(stack, factor, projection, work, packed, cross):
    squares = [stack[i * LANES : (i + 1) * LANES, :] for i in range(STACK // LANES)]
    work[:LANES, :LANES] = squares[0]
    work[:LANES, LANES:] = squares[1]
    work[LANES:, :LANES] = squares[1].T
    work[LANES:, LANES:] = squares[2]
    cross[:, :LANES] = squares[3]
    cross[:, LANES:] = squares[4]

    size = MEMBERS
    lanes = lax.broadcasted_iota(jnp.int32, (SUBLANES, LANES), 1)
    subs = lax.broadcasted_iota(jnp.int32, (SUBLANES, LANES), 0)
    groups = size // TILE
    halves = range(size // LANES)
    tiles = range(TILE // SUBLANES)

    def row_of(part, r):
        return jnp.broadcast_to(part[r : r + 1, :], (SUBLANES, LANES))

    def column_of(part, c):
        return jnp.broadcast_to(part[:, c : c + 1], (SUBLANES, LANES))

    def place_of(i, tile, half):
        start = i * TILE + tile * SUBLANES
        return slice(start, start + SUBLANES), slice(half * LANES, (half + 1) * LANES)

    def loaded(i):
        return [[work[place_of(i, t, h)] for h in halves] for t in tiles]

    def bf16_parts(values, order):
        parts = []
        for _ in range(3):
            part = values.astype(jnp.bfloat16).astype(jnp.float32)
            parts.append(part)
            values = values - part
        return jnp.concatenate([parts[k] for k in order], axis=0).astype(jnp.bfloat16)

    def whole(panel, first):
        return jnp.concatenate(
            [jnp.concatenate(panel[t][first:], axis=1) for t in tiles], axis=0
        )

    def cleared(part, start, count):
        return jnp.where((lanes >= start) & (lanes < start + count), 0.0, part)

    def total_of(terms):
        while len(terms) > 1:
            paired = [terms[k] + terms[k + 1] for k in range(0, len(terms) - 1, 2)]
            terms = paired + terms[len(terms) // 2 * 2 :]
        return terms[0]

    panel = loaded(0)
    update = None
    for group in range(groups):
        half, start = divmod(group * TILE, LANES)
        below = list(range(group + 1, groups))
        columns = [
            [[column_of(panel[t][half], start + r) for t in tiles] for r in range(SUBLANES)],
            [[column_of(panel[1][half], start + SUBLANES + r)] for r in range(SUBLANES)],
        ]

        def lowered(i):
            old = loaded(i)
            if update is None:
                return old
            values, first, last_half, last_start = update
            for t in tiles:
                for h in halves:
                    rows, cols = place_of(i, t, h)
                    if h == last_half:
                        old[t][h] = cleared(old[t][h], last_start, TILE)
                    old[t][h] = old[t][h] - values[rows.start - first : rows.stop - first, cols]
            return old

        following = lowered(below[0]) if below else None
        left = []
        right = []
        for tile in tiles:
            origin = start + tile * SUBLANES
            if below:
                entries = [
                    [column_of(following[t][half], origin + q) for t in tiles]
                    for q in range(SUBLANES)
                ]
            left.append(list(panel[tile]))
            taken = []
            for r in range(SUBLANES):
                column = columns[tile][r]
                at_row = subs == r
                at_lane = lanes == origin + r
                pivot = row_of(column[0], r)
                recip = 1.0 / pivot
                scale = lax.rsqrt(pivot)
                factor_of = [jnp.where(at_row, -1.0, column[0])] + column[1:]
                taken.append((column[-1], recip))

                def eliminated(parts, row):
                    kept = [jnp.where(at_row, 0.0, parts[0])] + parts[1:]
                    return [k - (f * row) * recip for k, f in zip(kept, factor_of)]

                for s in range(r + 1, SUBLANES):
                    columns[tile][s] = eliminated(columns[tile][s], row_of(columns[tile][s][0], r))
                index = group * TILE + tile * SUBLANES + r
                for h in halves:
                    parts = [panel[t][h] for t in tiles[tile:]]
                    row = row_of(parts[0], r)
                    if h == half:
                        row = jnp.where(at_lane, 1.0, row)
                        parts = [jnp.where(at_lane, 0.0, part) for part in parts]
                    packed[index : index + 1, h * LANES : (h + 1) * LANES] = (row * scale)[0:1]
                    for t, part in zip(tiles[tile:], eliminated(parts, row)):
                        panel[t][h] = part
                if update is not None:
                    for i in below[1 + tile * SUBLANES + r :: TILE]:
                        fresh = lowered(i)
                        for t in tiles:
                            for h in halves:
                                work[place_of(i, t, h)] = fresh[t][h]
            if tile == 0:
                columns[1] = [
                    [c[0] - total_of([v * (row_of(v, s) * recip) for v, recip in taken])]
                    for s, c in enumerate(columns[1])
                ]
            right.append(list(panel[tile]))
            if not below:
                continue
            solved = [[row_of(panel[tile][h], q) for h in halves] for q in range(SUBLANES)]
            for t in tiles:
                following[t][half] = cleared(following[t][half], origin, SUBLANES)
                for h in halves:
                    following[t][h] = following[t][h] - total_of(
                        [entries[q][t] * solved[q][h] for q in range(SUBLANES)]
                    )
        if below:
            right[0][half] = cleared(right[0][half], start + SUBLANES, SUBLANES)
            update = (
                transposed_product(
                    bf16_parts(whole(left, half), (0, 0, 0, 1, 1, 2)),
                    bf16_parts(whole(right, 0), (0, 1, 2, 0, 1, 0)),
                ),
                half * LANES,
                half,
                start,
            )
            panel = following

    row = lax.broadcasted_iota(jnp.int32, (size, size), 0)
    column = lax.broadcasted_iota(jnp.int32, (size, size), 1)
    result = packed[...]
    factor[...] = jnp.where(
        column > row, result, jnp.where(column == row, 1.0 / result, jnp.zeros_like(result))
    )
    inverse_t = jnp.where(column <= row, result, jnp.zeros_like(result)).astype(jnp.bfloat16)
    projection[...] = projected(cross[...], inverse_t)


def factor_and_projection(stack):
    return pl.pallas_call(
        factor_kernel,
        out_shape=(
            jax.ShapeDtypeStruct((MEMBERS, MEMBERS), jnp.float32),
            jax.ShapeDtypeStruct((MODES, MEMBERS), jnp.float32),
        ),
        in_specs=[VMEM],
        out_specs=(VMEM, VMEM),
        scratch_shapes=[
            pltpu.VMEM((MEMBERS, MEMBERS), jnp.float32),
            pltpu.VMEM((MEMBERS, MEMBERS), jnp.float32),
            pltpu.VMEM((MODES, MEMBERS), jnp.float32),
        ],
        name="factor_and_projection",
    )(stack)


def to_all(values, axes):
    count = lax.axis_size(axes)
    copies = jnp.broadcast_to(values[None], (count,) + values.shape)
    return lax.all_to_all(copies, axes, 0, 0)


def summed(stack):
    axes = ("y", "g")
    count = lax.axis_size(axes)
    pieces = stack.reshape(count, stack.shape[0] // count, LANES)
    piece = lax.all_to_all(pieces, axes, 0, 0).sum(0)
    piece = piece + lax.ppermute(piece, "c", [(0, 1), (1, 0)])
    piece = to_all(piece, "z").sum(0)
    return to_all(piece, axes).reshape(stack.shape)


def body(sensitivity, block_moves, shape_modes):
    panel = sensitivity[0]
    modes = shape_modes[0]
    moves = block_moves[0, 0]
    core = lax.axis_index("c").astype(jnp.int32).reshape(1)
    chain = ("y", "z", "c")
    count = lax.axis_size(chain)
    to_inner, to_outer = parcels(core, moves, panel, modes)
    pairs = range(1, count - 1, 2)
    outer = lax.ppermute(
        to_outer, chain, [(i, i + 1) for i in pairs] + [(i + 1, i) for i in pairs]
    )
    inner = lax.ppermute(to_inner, chain, [(i, i ^ 1) for i in range(count)])
    stack = own_rows(moves, panel, modes)
    stack, near, far = inner_edge(core, moves, panel, modes, inner, stack)
    stack = outer_edge(core, moves, near, far, outer, stack)
    return factor_and_projection(summed(stack))


def solution(mesh):
    split = Mesh(mesh.devices.reshape(4, 8, 2, 4), ("y", "z", "c", "g"))
    spec = P("g", ("y", "z", "c"), None)
    return jax.shard_map(
        body, mesh=split, in_specs=(spec, spec, spec), out_specs=(P(), P()), check_vma=False
    )
```

```python
import functools

import jax
import jax.numpy as jnp
from jax import lax
from jax.experimental import pallas as pl
from jax.experimental.pallas import tpu as pltpu
from jax.sharding import Mesh, PartitionSpec as P

BLOCK = 128
LANES = 128
MEMBERS = 256
MODES = 128
BLOCKS = 64
CHUNK = 32
CHUNK_ROWS = CHUNK * BLOCK
SUBLANES = 8
TILE = 16
STACK = 640
NEAR = 21
FAR = 11
NEAR_ROWS = NEAR * BLOCK
FAR_ROWS = FAR * BLOCK
PARCEL = 2 * FAR_ROWS
OUTER_PARCEL = PARCEL + 16
VMEM_BYTES = 51 * 1024 * 1024
EDGE_VMEM_BYTES = 45 * 1024 * 1024


def transposed_product(a, b):
    return lax.dot_general(a, b, (((0,), (0,)), ((), ())), preferred_element_type=jnp.float32)


def kept_blocks(values, first, start, stop):
    parts = []
    for index in range(values.shape[0] // BLOCK):
        part = values[index * BLOCK : (index + 1) * BLOCK, :]
        keep = (first + index >= start) & (first + index < stop)
        parts.append(jnp.where(keep, part, jnp.zeros_like(part)))
    return jnp.concatenate(parts, axis=0)


def block_rows(start, count):
    return pl.ds(pl.multiple_of(start * BLOCK, BLOCK), count * BLOCK)


def parcels_kernel(core, moves, panel, modes, to_inner, to_outer, sems):
    head, tail, prev, following = moves[0], moves[1], moves[2], moves[3]
    block_total = modes.shape[0] // BLOCK
    tail_start = head + block_total - prev - following
    second = core[0] != 0

    def far_copies(start, out, which):
        return [
            pltpu.make_async_copy(
                panel.at[block_rows(start, FAR), pl.ds(half * LANES, LANES)],
                out.at[pl.ds(half * FAR_ROWS, FAR_ROWS)],
                sems.at[which, half],
            )
            for half in range(2)
        ]

    def near_copies(start, out, which):
        return [
            pltpu.make_async_copy(
                modes.at[pl.ds(start * BLOCK, NEAR_ROWS)],
                out.at[pl.ds(0, NEAR_ROWS)],
                sems.at[which, 0],
            )
        ]

    choices = []
    for here, to_prev, to_next in (
        (second, to_inner, to_outer),
        (jnp.logical_not(second), to_outer, to_inner),
    ):
        choices += [
            (here & (head > 0), far_copies(0, to_prev, 0)),
            (here & (head == 0), near_copies(0, to_prev, 0)),
            (here & (tail > 0), far_copies(tail_start + NEAR, to_next, 1)),
            (here & (tail == 0), near_copies(block_total - NEAR, to_next, 1)),
        ]
    for chosen, copies in choices:

        @pl.when(chosen)
        def _():
            for copy in copies:
                copy.start()

    for chosen, copies in choices:

        @pl.when(chosen)
        def _():
            for copy in copies:
                copy.wait()


def own_rows_kernel(
    moves, panel, modes, out, panel_v, modes_v, gram, cross, panel_sem, modes_sem
):
    head, tail, prev, following = moves[0], moves[1], moves[2], moves[3]
    block_total = modes.shape[0] // BLOCK
    lead = block_total // 2
    own = block_total - prev - following
    valid = head + own + tail
    steps = jnp.maximum(lax.div(valid + (CHUNK - 1), CHUNK), 1)

    def panel_copy(i):
        rows = block_rows(i * CHUNK, CHUNK)
        return pltpu.make_async_copy(panel.at[rows], panel_v.at[rows], panel_sem.at[i])

    modes_copy = pltpu.make_async_copy(
        modes, modes_v.at[block_rows(lead + head - prev, block_total)], modes_sem
    )
    panel_copy(0).start()
    modes_copy.start()

    def launch(i, carry):
        panel_copy(i).start()
        return carry

    lax.fori_loop(1, steps, launch, 0)
    gram[...] = jnp.zeros_like(gram)
    cross[...] = jnp.zeros_like(cross)
    modes_copy.wait()

    def step(i, carry):
        panel_copy(i).wait()
        block = i * CHUNK
        values = panel_v[block_rows(block, CHUNK), :]
        beside = modes_v[block_rows(block + lead, CHUNK), :]
        gram[...] += transposed_product(values, kept_blocks(values, block, 0, valid))
        cross[...] += transposed_product(kept_blocks(beside, block, head, head + own), values)
        return carry

    lax.fori_loop(0, steps, step, 0)
    out[:LANES, :] = gram[:LANES, :LANES]
    out[LANES : 2 * LANES, :] = gram[:LANES, LANES:]
    out[2 * LANES : 3 * LANES, :] = gram[LANES:, LANES:]
    for i in range(2):
        out[(3 + i) * LANES : (4 + i) * LANES, :] = cross[:, i * LANES : (i + 1) * LANES]


class Edge:
    def __init__(self, from_prev, moves, block_total):
        head, tail, prev, following = moves[0], moves[1], moves[2], moves[3]
        own = block_total - prev - following
        far_start = jnp.minimum(block_total - following, block_total - FAR)
        self.near = jnp.where(from_prev, head, tail)
        self.near_source = jnp.where(from_prev, jnp.maximum(head - NEAR, 0), head + own)
        self.near_offset = jnp.where(from_prev, jnp.minimum(head, NEAR), NEAR)
        self.near_first = jnp.where(from_prev, NEAR - head, 0)
        self.near_stop = jnp.where(from_prev, NEAR, tail)
        self.far = jnp.where(from_prev, prev, following) - NEAR
        self.far_source = jnp.where(from_prev, NEAR, far_start)

    def copies(self, panel, modes, near_v, far_v, sems):
        near = pltpu.make_async_copy(
            panel.at[block_rows(self.near_source, NEAR)],
            near_v.at[pl.ds(NEAR_ROWS, NEAR_ROWS)],
            sems.at[0],
        )
        far = pltpu.make_async_copy(
            modes.at[block_rows(self.far_source, FAR)], far_v, sems.at[1]
        )
        return [(self.near > 0, near), (self.far > 0, far)]

    def multiply(self, near_v, far_v, parcel, out):
        def add(index, values):
            out[index * LANES : (index + 1) * LANES, :] += values

        @pl.when(self.near > 0)
        def _():
            mode_values = kept_blocks(parcel[:NEAR_ROWS, :], 0, self.near_first, self.near_stop)
            panel_values = near_v[block_rows(self.near_offset, NEAR), :]
            product = transposed_product(mode_values, panel_values)
            for i in range(2):
                add(3 + i, product[:, i * LANES : (i + 1) * LANES])

        @pl.when(self.far > 0)
        def _():
            mode_values = kept_blocks(far_v[...], 0, 0, self.far)
            for i in range(2):
                values = parcel[i * FAR_ROWS : (i + 1) * FAR_ROWS, :]
                add(3 + i, transposed_product(mode_values, values))


def inner_edge_kernel(
    core, moves, panel, modes, parcel, before, out, outer_near, outer_far, near_v, far_v, sems
):
    block_total = modes.shape[0] // BLOCK
    inner = Edge(core[0] != 0, moves, block_total)
    outer = Edge(core[0] == 0, moves, block_total)
    inner_copies = inner.copies(panel, modes, near_v, far_v, sems.at[0])
    outer_copies = outer.copies(panel, modes, outer_near, outer_far, sems.at[1])
    for needed, copy in inner_copies + outer_copies:
        pl.when(needed)(copy.start)
    filler = jnp.zeros((NEAR_ROWS, MEMBERS), near_v.dtype)
    near_v[:NEAR_ROWS, :] = filler
    outer_near[:NEAR_ROWS, :] = filler
    out[...] = before[...]
    for needed, copy in inner_copies:
        pl.when(needed)(copy.wait)
    inner.multiply(near_v, far_v, parcel, out)
    for needed, copy in outer_copies:
        pl.when(needed)(copy.wait)


def outer_edge_kernel(core, moves, outer_near, outer_far, parcel, before, out):
    outer = Edge(core[0] == 0, moves, BLOCKS)
    out[...] = before[...]
    outer.multiply(outer_near, outer_far, parcel, out)


SMEM = pl.BlockSpec(memory_space=pltpu.SMEM)
VMEM = pl.BlockSpec(memory_space=pltpu.VMEM)
HBM = pl.BlockSpec(memory_space=pltpu.HBM)


def parcels(core, moves, panel, modes):
    return pl.pallas_call(
        parcels_kernel,
        out_shape=(
            jax.ShapeDtypeStruct((PARCEL, LANES), modes.dtype),
            jax.ShapeDtypeStruct((OUTER_PARCEL, LANES), modes.dtype),
        ),
        in_specs=[SMEM, SMEM, HBM, HBM],
        out_specs=(VMEM, VMEM),
        scratch_shapes=[pltpu.SemaphoreType.DMA((2, 2))],
        compiler_params=pltpu.CompilerParams(vmem_limit_bytes=VMEM_BYTES),
        cost_estimate=pl.CostEstimate(flops=0, bytes_accessed=3 * 1024 * 1024, transcendentals=0),
        name="parcels",
    )(core, moves, panel, modes)


def own_rows(moves, panel, modes):
    slots = panel.shape[0] // BLOCK
    return pl.pallas_call(
        own_rows_kernel,
        out_shape=jax.ShapeDtypeStruct((STACK, LANES), jnp.float32),
        in_specs=[SMEM, HBM, HBM],
        out_specs=VMEM,
        scratch_shapes=[
            pltpu.VMEM(panel.shape, panel.dtype),
            pltpu.VMEM((panel.shape[0] + modes.shape[0] // 2, MODES), modes.dtype),
            pltpu.VMEM((MEMBERS, MEMBERS), jnp.float32),
            pltpu.VMEM((MODES, MEMBERS), jnp.float32),
            pltpu.SemaphoreType.DMA((slots // CHUNK,)),
            pltpu.SemaphoreType.DMA,
        ],
        compiler_params=pltpu.CompilerParams(vmem_limit_bytes=VMEM_BYTES),
        cost_estimate=pl.CostEstimate(
            flops=2 * 12288 * 384 * 256, bytes_accessed=10 * 1024 * 1024, transcendentals=0
        ),
        name="own_rows",
    )(moves, panel, modes)


def inner_edge(core, moves, panel, modes, parcel, before):
    near = (2 * NEAR_ROWS, MEMBERS)
    far = (FAR_ROWS, MODES)
    return pl.pallas_call(
        inner_edge_kernel,
        out_shape=(
            jax.ShapeDtypeStruct((STACK, LANES), jnp.float32),
            jax.ShapeDtypeStruct(near, panel.dtype),
            jax.ShapeDtypeStruct(far, modes.dtype),
        ),
        in_specs=[SMEM, SMEM, HBM, HBM, VMEM, VMEM],
        out_specs=(VMEM, VMEM, VMEM),
        scratch_shapes=[
            pltpu.VMEM(near, panel.dtype),
            pltpu.VMEM(far, modes.dtype),
            pltpu.SemaphoreType.DMA((2, 2)),
        ],
        compiler_params=pltpu.CompilerParams(vmem_limit_bytes=EDGE_VMEM_BYTES),
        cost_estimate=pl.CostEstimate(
            flops=0, bytes_accessed=1024, transcendentals=0
        ),
        name="inner_edge",
    )(core, moves, panel, modes, parcel, before)


def outer_edge(core, moves, near, far, parcel, before):
    return pl.pallas_call(
        outer_edge_kernel,
        out_shape=jax.ShapeDtypeStruct((STACK, LANES), jnp.float32),
        in_specs=[SMEM, SMEM, VMEM, VMEM, VMEM, VMEM],
        out_specs=VMEM,
        compiler_params=pltpu.CompilerParams(vmem_limit_bytes=EDGE_VMEM_BYTES),
        cost_estimate=pl.CostEstimate(
            flops=0, bytes_accessed=1024, transcendentals=0
        ),
        name="outer_edge",
    )(core, moves, near, far, parcel, before)


def projected(product, inverse_t):
    high = product.astype(jnp.bfloat16)
    rest = product - high.astype(jnp.float32)
    middle = rest.astype(jnp.bfloat16)
    low = (rest - middle.astype(jnp.float32)).astype(jnp.bfloat16)

    def part(values):
        return lax.dot_general(
            values, inverse_t, (((1,), (1,)), ((), ())), preferred_element_type=jnp.float32
        )

    return part(low) + part(middle) + part(high)


def factor_kernel(stack, factor, projection, work, packed, cross):
    squares = [stack[i * LANES : (i + 1) * LANES, :] for i in range(STACK // LANES)]
    work[:LANES, :LANES] = squares[0]
    work[:LANES, LANES:] = squares[1]
    work[LANES:, :LANES] = squares[1].T
    work[LANES:, LANES:] = squares[2]
    cross[:, :LANES] = squares[3]
    cross[:, LANES:] = squares[4]

    size = MEMBERS
    lanes = lax.broadcasted_iota(jnp.int32, (SUBLANES, LANES), 1)
    subs = lax.broadcasted_iota(jnp.int32, (SUBLANES, LANES), 0)
    groups = size // TILE
    halves = range(size // LANES)
    tiles = range(TILE // SUBLANES)

    def row_of(part, r):
        return jnp.broadcast_to(part[r : r + 1, :], (SUBLANES, LANES))

    def column_of(part, c):
        return jnp.broadcast_to(part[:, c : c + 1], (SUBLANES, LANES))

    def place_of(i, tile, half):
        start = i * TILE + tile * SUBLANES
        return slice(start, start + SUBLANES), slice(half * LANES, (half + 1) * LANES)

    def loaded(i):
        return [[work[place_of(i, t, h)] for h in halves] for t in tiles]

    def bf16_parts(values, order):
        parts = []
        for _ in range(3):
            part = values.astype(jnp.bfloat16).astype(jnp.float32)
            parts.append(part)
            values = values - part
        return jnp.concatenate([parts[k] for k in order], axis=0).astype(jnp.bfloat16)

    def whole(panel, first):
        return jnp.concatenate(
            [jnp.concatenate(panel[t][first:], axis=1) for t in tiles], axis=0
        )

    def cleared(part, start, count):
        return jnp.where((lanes >= start) & (lanes < start + count), 0.0, part)

    def total_of(terms):
        while len(terms) > 1:
            paired = [terms[k] + terms[k + 1] for k in range(0, len(terms) - 1, 2)]
            terms = paired + terms[len(terms) // 2 * 2 :]
        return terms[0]

    panel = loaded(0)
    update = None
    for group in range(groups):
        half, start = divmod(group * TILE, LANES)
        below = list(range(group + 1, groups))
        columns = [
            [[column_of(panel[t][half], start + r) for t in tiles] for r in range(SUBLANES)],
            [[column_of(panel[1][half], start + SUBLANES + r)] for r in range(SUBLANES)],
        ]

        def lowered(i):
            old = loaded(i)
            if update is None:
                return old
            values, first, last_half, last_start = update
            for t in tiles:
                for h in halves:
                    rows, cols = place_of(i, t, h)
                    if h == last_half:
                        old[t][h] = cleared(old[t][h], last_start, TILE)
                    old[t][h] = old[t][h] - values[rows.start - first : rows.stop - first, cols]
            return old

        following = lowered(below[0]) if below else None
        left = []
        right = []
        for tile in tiles:
            origin = start + tile * SUBLANES
            if below:
                entries = [
                    [column_of(following[t][half], origin + q) for t in tiles]
                    for q in range(SUBLANES)
                ]
            left.append(list(panel[tile]))
            taken = []
            for r in range(SUBLANES):
                column = columns[tile][r]
                at_row = subs == r
                at_lane = lanes == origin + r
                pivot = row_of(column[0], r)
                recip = 1.0 / pivot
                scale = lax.rsqrt(pivot)
                factor_of = [jnp.where(at_row, -1.0, column[0])] + column[1:]
                taken.append((column[-1], recip))

                def eliminated(parts, row):
                    kept = [jnp.where(at_row, 0.0, parts[0])] + parts[1:]
                    return [k - (f * row) * recip for k, f in zip(kept, factor_of)]

                for s in range(r + 1, SUBLANES):
                    columns[tile][s] = eliminated(columns[tile][s], row_of(columns[tile][s][0], r))
                index = group * TILE + tile * SUBLANES + r
                for h in halves:
                    parts = [panel[t][h] for t in tiles[tile:]]
                    row = row_of(parts[0], r)
                    if h == half:
                        row = jnp.where(at_lane, 1.0, row)
                        parts = [jnp.where(at_lane, 0.0, part) for part in parts]
                    packed[index : index + 1, h * LANES : (h + 1) * LANES] = (row * scale)[0:1]
                    for t, part in zip(tiles[tile:], eliminated(parts, row)):
                        panel[t][h] = part
                if update is not None:
                    for i in below[1 + tile * SUBLANES + r :: TILE]:
                        fresh = lowered(i)
                        for t in tiles:
                            for h in halves:
                                work[place_of(i, t, h)] = fresh[t][h]
            if tile == 0:
                columns[1] = [
                    [c[0] - total_of([v * (row_of(v, s) * recip) for v, recip in taken])]
                    for s, c in enumerate(columns[1])
                ]
            right.append(list(panel[tile]))
            if not below:
                continue
            solved = [[row_of(panel[tile][h], q) for h in halves] for q in range(SUBLANES)]
            for t in tiles:
                following[t][half] = cleared(following[t][half], origin, SUBLANES)
                for h in halves:
                    following[t][h] = following[t][h] - total_of(
                        [entries[q][t] * solved[q][h] for q in range(SUBLANES)]
                    )
        if below:
            right[0][half] = cleared(right[0][half], start + SUBLANES, SUBLANES)
            update = (
                transposed_product(
                    bf16_parts(whole(left, half), (0, 0, 0, 1, 1, 2)),
                    bf16_parts(whole(right, 0), (0, 1, 2, 0, 1, 0)),
                ),
                half * LANES,
                half,
                start,
            )
            panel = following

    row = lax.broadcasted_iota(jnp.int32, (size, size), 0)
    column = lax.broadcasted_iota(jnp.int32, (size, size), 1)
    result = packed[...]
    factor[...] = jnp.where(
        column > row, result, jnp.where(column == row, 1.0 / result, jnp.zeros_like(result))
    )
    inverse_t = jnp.where(column <= row, result, jnp.zeros_like(result)).astype(jnp.bfloat16)
    projection[...] = projected(cross[...], inverse_t)


def factor_and_projection(stack):
    return pl.pallas_call(
        factor_kernel,
        out_shape=(
            jax.ShapeDtypeStruct((MEMBERS, MEMBERS), jnp.float32),
            jax.ShapeDtypeStruct((MODES, MEMBERS), jnp.float32),
        ),
        in_specs=[VMEM],
        out_specs=(VMEM, VMEM),
        scratch_shapes=[
            pltpu.VMEM((MEMBERS, MEMBERS), jnp.float32),
            pltpu.VMEM((MEMBERS, MEMBERS), jnp.float32),
            pltpu.VMEM((MODES, MEMBERS), jnp.float32),
        ],
        name="factor_and_projection",
    )(stack)


def to_all(values, axes):
    count = lax.axis_size(axes)
    copies = jnp.broadcast_to(values[None], (count,) + values.shape)
    return lax.all_to_all(copies, axes, 0, 0)


def summed(stack):
    axes = ("y", "g")
    count = lax.axis_size(axes)
    pieces = stack.reshape(count, stack.shape[0] // count, LANES)
    piece = lax.all_to_all(pieces, axes, 0, 0).sum(0)
    piece = piece + lax.ppermute(piece, "c", [(0, 1), (1, 0)])
    piece = to_all(piece, "z").sum(0)
    return to_all(piece, axes).reshape(stack.shape)


def body(sensitivity, block_moves, shape_modes):
    panel = sensitivity[0]
    modes = shape_modes[0]
    moves = block_moves[0, 0]
    core = lax.axis_index("c").astype(jnp.int32).reshape(1)
    chain = ("y", "z", "c")
    count = lax.axis_size(chain)
    to_inner, to_outer = parcels(core, moves, panel, modes)
    pairs = range(1, count - 1, 2)
    outer = lax.ppermute(
        to_outer, chain, [(i, i + 1) for i in pairs] + [(i + 1, i) for i in pairs]
    )
    inner = lax.ppermute(to_inner, chain, [(i, i ^ 1) for i in range(count)])
    stack = own_rows(moves, panel, modes)
    stack, near, far = inner_edge(core, moves, panel, modes, inner, stack)
    stack = outer_edge(core, moves, near, far, outer, stack)
    return factor_and_projection(summed(stack))


def solution(mesh):
    split = Mesh(mesh.devices.reshape(4, 8, 2, 4), ("y", "z", "c", "g"))
    spec = P("g", ("y", "z", "c"), None)
    return jax.shard_map(
        body, mesh=split, in_specs=(spec, spec, spec), out_specs=(P(), P()), check_vma=False
    )
```

```python
import functools

import jax
import jax.numpy as jnp
from jax import lax
from jax.experimental import pallas as pl
from jax.experimental.pallas import tpu as pltpu
from jax.sharding import Mesh, PartitionSpec as P

BLOCK = 128
LANES = 128
MEMBERS = 256
MODES = 128
BLOCKS = 64
CHUNK = 32
CHUNK_ROWS = CHUNK * BLOCK
SUBLANES = 8
TILE = 16
STACK = 640
NEAR = 21
FAR = 11
NEAR_ROWS = NEAR * BLOCK
FAR_ROWS = FAR * BLOCK
PARCEL = 2 * FAR_ROWS
OUTER_PARCEL = PARCEL + 16
VMEM_BYTES = 51 * 1024 * 1024
EDGE_VMEM_BYTES = 45 * 1024 * 1024


def transposed_product(a, b):
    return lax.dot_general(a, b, (((0,), (0,)), ((), ())), preferred_element_type=jnp.float32)


def kept_blocks(values, first, start, stop):
    parts = []
    for index in range(values.shape[0] // BLOCK):
        part = values[index * BLOCK : (index + 1) * BLOCK, :]
        keep = (first + index >= start) & (first + index < stop)
        parts.append(jnp.where(keep, part, jnp.zeros_like(part)))
    return jnp.concatenate(parts, axis=0)


def block_rows(start, count):
    return pl.ds(pl.multiple_of(start * BLOCK, BLOCK), count * BLOCK)


def parcels_kernel(core, moves, panel, modes, to_inner, to_outer, sems):
    head, tail, prev, following = moves[0], moves[1], moves[2], moves[3]
    block_total = modes.shape[0] // BLOCK
    tail_start = head + block_total - prev - following
    second = core[0] != 0

    def far_copies(start, out, which):
        return [
            pltpu.make_async_copy(
                panel.at[block_rows(start, FAR), pl.ds(half * LANES, LANES)],
                out.at[pl.ds(half * FAR_ROWS, FAR_ROWS)],
                sems.at[which, half],
            )
            for half in range(2)
        ]

    def near_copies(start, out, which):
        return [
            pltpu.make_async_copy(
                modes.at[pl.ds(start * BLOCK, NEAR_ROWS)],
                out.at[pl.ds(0, NEAR_ROWS)],
                sems.at[which, 0],
            )
        ]

    choices = []
    for here, to_prev, to_next in (
        (second, to_inner, to_outer),
        (jnp.logical_not(second), to_outer, to_inner),
    ):
        choices += [
            (here & (head > 0), far_copies(0, to_prev, 0)),
            (here & (head == 0), near_copies(0, to_prev, 0)),
            (here & (tail > 0), far_copies(tail_start + NEAR, to_next, 1)),
            (here & (tail == 0), near_copies(block_total - NEAR, to_next, 1)),
        ]
    for chosen, copies in choices:

        @pl.when(chosen)
        def _():
            for copy in copies:
                copy.start()

    for chosen, copies in choices:

        @pl.when(chosen)
        def _():
            for copy in copies:
                copy.wait()


def own_rows_kernel(
    moves, panel, modes, out, panel_v, modes_v, gram, cross, panel_sem, modes_sem
):
    head, tail, prev, following = moves[0], moves[1], moves[2], moves[3]
    block_total = modes.shape[0] // BLOCK
    lead = block_total // 2
    own = block_total - prev - following
    valid = head + own + tail
    steps = jnp.maximum(lax.div(valid + (CHUNK - 1), CHUNK), 1)

    def panel_copy(i):
        rows = block_rows(i * CHUNK, CHUNK)
        return pltpu.make_async_copy(panel.at[rows], panel_v.at[rows], panel_sem.at[i])

    modes_copy = pltpu.make_async_copy(
        modes, modes_v.at[block_rows(lead + head - prev, block_total)], modes_sem
    )
    panel_copy(0).start()
    modes_copy.start()

    def launch(i, carry):
        panel_copy(i).start()
        return carry

    lax.fori_loop(1, steps, launch, 0)
    gram[...] = jnp.zeros_like(gram)
    cross[...] = jnp.zeros_like(cross)
    modes_copy.wait()

    def step(i, carry):
        panel_copy(i).wait()
        block = i * CHUNK
        values = panel_v[block_rows(block, CHUNK), :]
        beside = modes_v[block_rows(block + lead, CHUNK), :]
        gram[...] += transposed_product(values, kept_blocks(values, block, 0, valid))
        cross[...] += transposed_product(kept_blocks(beside, block, head, head + own), values)
        return carry

    lax.fori_loop(0, steps, step, 0)
    out[:LANES, :] = gram[:LANES, :LANES]
    out[LANES : 2 * LANES, :] = gram[:LANES, LANES:]
    out[2 * LANES : 3 * LANES, :] = gram[LANES:, LANES:]
    for i in range(2):
        out[(3 + i) * LANES : (4 + i) * LANES, :] = cross[:, i * LANES : (i + 1) * LANES]


class Edge:
    def __init__(self, from_prev, moves, block_total):
        head, tail, prev, following = moves[0], moves[1], moves[2], moves[3]
        own = block_total - prev - following
        far_start = jnp.minimum(block_total - following, block_total - FAR)
        self.near = jnp.where(from_prev, head, tail)
        self.near_source = jnp.where(from_prev, jnp.maximum(head - NEAR, 0), head + own)
        self.near_offset = jnp.where(from_prev, jnp.minimum(head, NEAR), NEAR)
        self.near_first = jnp.where(from_prev, NEAR - head, 0)
        self.near_stop = jnp.where(from_prev, NEAR, tail)
        self.far = jnp.where(from_prev, prev, following) - NEAR
        self.far_source = jnp.where(from_prev, NEAR, far_start)

    def copies(self, panel, modes, near_v, far_v, sems):
        near = pltpu.make_async_copy(
            panel.at[block_rows(self.near_source, NEAR)],
            near_v.at[pl.ds(NEAR_ROWS, NEAR_ROWS)],
            sems.at[0],
        )
        far = pltpu.make_async_copy(
            modes.at[block_rows(self.far_source, FAR)], far_v, sems.at[1]
        )
        return [(self.near > 0, near), (self.far > 0, far)]

    def multiply(self, near_v, far_v, parcel, out):
        def add(index, values):
            out[index * LANES : (index + 1) * LANES, :] += values

        @pl.when(self.near > 0)
        def _():
            mode_values = kept_blocks(parcel[:NEAR_ROWS, :], 0, self.near_first, self.near_stop)
            panel_values = near_v[block_rows(self.near_offset, NEAR), :]
            product = transposed_product(mode_values, panel_values)
            for i in range(2):
                add(3 + i, product[:, i * LANES : (i + 1) * LANES])

        @pl.when(self.far > 0)
        def _():
            mode_values = kept_blocks(far_v[...], 0, 0, self.far)
            for i in range(2):
                values = parcel[i * FAR_ROWS : (i + 1) * FAR_ROWS, :]
                add(3 + i, transposed_product(mode_values, values))


def inner_edge_kernel(
    core, moves, panel, modes, parcel, before, out, outer_near, outer_far, near_v, far_v, sems
):
    block_total = modes.shape[0] // BLOCK
    inner = Edge(core[0] != 0, moves, block_total)
    outer = Edge(core[0] == 0, moves, block_total)
    inner_copies = inner.copies(panel, modes, near_v, far_v, sems.at[0])
    outer_copies = outer.copies(panel, modes, outer_near, outer_far, sems.at[1])
    for needed, copy in inner_copies + outer_copies:
        pl.when(needed)(copy.start)
    filler = jnp.zeros((NEAR_ROWS, MEMBERS), near_v.dtype)
    near_v[:NEAR_ROWS, :] = filler
    outer_near[:NEAR_ROWS, :] = filler
    out[...] = before[...]
    for needed, copy in inner_copies:
        pl.when(needed)(copy.wait)
    inner.multiply(near_v, far_v, parcel, out)
    for needed, copy in outer_copies:
        pl.when(needed)(copy.wait)


def outer_edge_kernel(core, moves, outer_near, outer_far, parcel, before, out):
    outer = Edge(core[0] == 0, moves, BLOCKS)
    out[...] = before[...]
    outer.multiply(outer_near, outer_far, parcel, out)


SMEM = pl.BlockSpec(memory_space=pltpu.SMEM)
VMEM = pl.BlockSpec(memory_space=pltpu.VMEM)
HBM = pl.BlockSpec(memory_space=pltpu.HBM)


def parcels(core, moves, panel, modes):
    return pl.pallas_call(
        parcels_kernel,
        out_shape=(
            jax.ShapeDtypeStruct((PARCEL, LANES), modes.dtype),
            jax.ShapeDtypeStruct((OUTER_PARCEL, LANES), modes.dtype),
        ),
        in_specs=[SMEM, SMEM, HBM, HBM],
        out_specs=(VMEM, VMEM),
        scratch_shapes=[pltpu.SemaphoreType.DMA((2, 2))],
        compiler_params=pltpu.CompilerParams(vmem_limit_bytes=VMEM_BYTES),
        cost_estimate=pl.CostEstimate(flops=0, bytes_accessed=3 * 1024 * 1024, transcendentals=0),
        name="parcels",
    )(core, moves, panel, modes)


def own_rows(moves, panel, modes):
    slots = panel.shape[0] // BLOCK
    return pl.pallas_call(
        own_rows_kernel,
        out_shape=jax.ShapeDtypeStruct((STACK, LANES), jnp.float32),
        in_specs=[SMEM, HBM, HBM],
        out_specs=VMEM,
        scratch_shapes=[
            pltpu.VMEM(panel.shape, panel.dtype),
            pltpu.VMEM((panel.shape[0] + modes.shape[0] // 2, MODES), modes.dtype),
            pltpu.VMEM((MEMBERS, MEMBERS), jnp.float32),
            pltpu.VMEM((MODES, MEMBERS), jnp.float32),
            pltpu.SemaphoreType.DMA((slots // CHUNK,)),
            pltpu.SemaphoreType.DMA,
        ],
        compiler_params=pltpu.CompilerParams(vmem_limit_bytes=VMEM_BYTES),
        cost_estimate=pl.CostEstimate(
            flops=2 * 12288 * 384 * 256, bytes_accessed=10 * 1024 * 1024, transcendentals=0
        ),
        name="own_rows",
    )(moves, panel, modes)


def inner_edge(core, moves, panel, modes, parcel, before):
    near = (2 * NEAR_ROWS, MEMBERS)
    far = (FAR_ROWS, MODES)
    return pl.pallas_call(
        inner_edge_kernel,
        out_shape=(
            jax.ShapeDtypeStruct((STACK, LANES), jnp.float32),
            jax.ShapeDtypeStruct(near, panel.dtype),
            jax.ShapeDtypeStruct(far, modes.dtype),
        ),
        in_specs=[SMEM, SMEM, HBM, HBM, VMEM, VMEM],
        out_specs=(VMEM, VMEM, VMEM),
        scratch_shapes=[
            pltpu.VMEM(near, panel.dtype),
            pltpu.VMEM(far, modes.dtype),
            pltpu.SemaphoreType.DMA((2, 2)),
        ],
        compiler_params=pltpu.CompilerParams(vmem_limit_bytes=EDGE_VMEM_BYTES),
        cost_estimate=pl.CostEstimate(
            flops=0, bytes_accessed=1024, transcendentals=0
        ),
        name="inner_edge",
    )(core, moves, panel, modes, parcel, before)


def outer_edge(core, moves, near, far, parcel, before):
    return pl.pallas_call(
        outer_edge_kernel,
        out_shape=jax.ShapeDtypeStruct((STACK, LANES), jnp.float32),
        in_specs=[SMEM, SMEM, VMEM, VMEM, VMEM, VMEM],
        out_specs=VMEM,
        compiler_params=pltpu.CompilerParams(vmem_limit_bytes=EDGE_VMEM_BYTES),
        cost_estimate=pl.CostEstimate(
            flops=0, bytes_accessed=1024, transcendentals=0
        ),
        name="outer_edge",
    )(core, moves, near, far, parcel, before)


def projected(product, inverse_t):
    high = product.astype(jnp.bfloat16)
    rest = product - high.astype(jnp.float32)
    middle = rest.astype(jnp.bfloat16)
    low = (rest - middle.astype(jnp.float32)).astype(jnp.bfloat16)

    def part(values):
        return lax.dot_general(
            values, inverse_t, (((1,), (1,)), ((), ())), preferred_element_type=jnp.float32
        )

    return part(low) + part(middle) + part(high)


def factor_kernel(stack, factor, projection, work, packed, cross):
    squares = [stack[i * LANES : (i + 1) * LANES, :] for i in range(STACK // LANES)]
    work[:LANES, :LANES] = squares[0]
    work[:LANES, LANES:] = squares[1]
    work[LANES:, :LANES] = squares[1].T
    work[LANES:, LANES:] = squares[2]
    cross[:, :LANES] = squares[3]
    cross[:, LANES:] = squares[4]

    size = MEMBERS
    lanes = lax.broadcasted_iota(jnp.int32, (SUBLANES, LANES), 1)
    subs = lax.broadcasted_iota(jnp.int32, (SUBLANES, LANES), 0)
    groups = size // TILE
    halves = range(size // LANES)
    tiles = range(TILE // SUBLANES)

    def row_of(part, r):
        return jnp.broadcast_to(part[r : r + 1, :], (SUBLANES, LANES))

    def column_of(part, c):
        return jnp.broadcast_to(part[:, c : c + 1], (SUBLANES, LANES))

    def place_of(i, tile, half):
        start = i * TILE + tile * SUBLANES
        return slice(start, start + SUBLANES), slice(half * LANES, (half + 1) * LANES)

    def loaded(i):
        return [[work[place_of(i, t, h)] for h in halves] for t in tiles]

    def bf16_parts(values, order):
        parts = []
        for _ in range(3):
            part = values.astype(jnp.bfloat16).astype(jnp.float32)
            parts.append(part)
            values = values - part
        return jnp.concatenate([parts[k] for k in order], axis=0).astype(jnp.bfloat16)

    def whole(panel, first):
        return jnp.concatenate(
            [jnp.concatenate(panel[t][first:], axis=1) for t in tiles], axis=0
        )

    def cleared(part, start, count):
        return jnp.where((lanes >= start) & (lanes < start + count), 0.0, part)

    def total_of(terms):
        while len(terms) > 1:
            paired = [terms[k] + terms[k + 1] for k in range(0, len(terms) - 1, 2)]
            terms = paired + terms[len(terms) // 2 * 2 :]
        return terms[0]

    panel = loaded(0)
    update = None
    for group in range(groups):
        half, start = divmod(group * TILE, LANES)
        below = list(range(group + 1, groups))
        columns = [
            [[column_of(panel[t][half], start + r) for t in tiles] for r in range(SUBLANES)],
            [[column_of(panel[1][half], start + SUBLANES + r)] for r in range(SUBLANES)],
        ]

        def lowered(i):
            old = loaded(i)
            if update is None:
                return old
            values, first, last_half, last_start = update
            for t in tiles:
                for h in halves:
                    rows, cols = place_of(i, t, h)
                    if h == last_half:
                        old[t][h] = cleared(old[t][h], last_start, TILE)
                    old[t][h] = old[t][h] - values[rows.start - first : rows.stop - first, cols]
            return old

        following = lowered(below[0]) if below else None
        left = []
        right = []
        for tile in tiles:
            origin = start + tile * SUBLANES
            if below:
                entries = [
                    [column_of(following[t][half], origin + q) for t in tiles]
                    for q in range(SUBLANES)
                ]
            left.append(list(panel[tile]))
            taken = []
            for r in range(SUBLANES):
                column = columns[tile][r]
                at_row = subs == r
                at_lane = lanes == origin + r
                pivot = row_of(column[0], r)
                recip = 1.0 / pivot
                scale = lax.rsqrt(pivot)
                factor_of = [jnp.where(at_row, -1.0, column[0])] + column[1:]
                taken.append((column[-1], recip))

                def eliminated(parts, row):
                    kept = [jnp.where(at_row, 0.0, parts[0])] + parts[1:]
                    return [k - (f * row) * recip for k, f in zip(kept, factor_of)]

                for s in range(r + 1, SUBLANES):
                    columns[tile][s] = eliminated(columns[tile][s], row_of(columns[tile][s][0], r))
                index = group * TILE + tile * SUBLANES + r
                for h in halves:
                    parts = [panel[t][h] for t in tiles[tile:]]
                    row = row_of(parts[0], r)
                    if h == half:
                        row = jnp.where(at_lane, 1.0, row)
                        parts = [jnp.where(at_lane, 0.0, part) for part in parts]
                    packed[index : index + 1, h * LANES : (h + 1) * LANES] = (row * scale)[0:1]
                    for t, part in zip(tiles[tile:], eliminated(parts, row)):
                        panel[t][h] = part
                if update is not None:
                    for i in below[1 + tile * SUBLANES + r :: TILE]:
                        fresh = lowered(i)
                        for t in tiles:
                            for h in halves:
                                work[place_of(i, t, h)] = fresh[t][h]
            if tile == 0:
                columns[1] = [
                    [c[0] - total_of([v * (row_of(v, s) * recip) for v, recip in taken])]
                    for s, c in enumerate(columns[1])
                ]
            right.append(list(panel[tile]))
            if not below:
                continue
            solved = [[row_of(panel[tile][h], q) for h in halves] for q in range(SUBLANES)]
            for t in tiles:
                following[t][half] = cleared(following[t][half], origin, SUBLANES)
                for h in halves:
                    following[t][h] = following[t][h] - total_of(
                        [entries[q][t] * solved[q][h] for q in range(SUBLANES)]
                    )
        if below:
            right[0][half] = cleared(right[0][half], start + SUBLANES, SUBLANES)
            update = (
                transposed_product(
                    bf16_parts(whole(left, half), (0, 0, 0, 1, 1, 2)),
                    bf16_parts(whole(right, 0), (0, 1, 2, 0, 1, 0)),
                ),
                half * LANES,
                half,
                start,
            )
            panel = following

    row = lax.broadcasted_iota(jnp.int32, (size, size), 0)
    column = lax.broadcasted_iota(jnp.int32, (size, size), 1)
    result = packed[...]
    factor[...] = jnp.where(
        column > row, result, jnp.where(column == row, 1.0 / result, jnp.zeros_like(result))
    )
    inverse_t = jnp.where(column <= row, result, jnp.zeros_like(result)).astype(jnp.bfloat16)
    projection[...] = projected(cross[...], inverse_t)


def factor_and_projection(stack):
    return pl.pallas_call(
        factor_kernel,
        out_shape=(
            jax.ShapeDtypeStruct((MEMBERS, MEMBERS), jnp.float32),
            jax.ShapeDtypeStruct((MODES, MEMBERS), jnp.float32),
        ),
        in_specs=[VMEM],
        out_specs=(VMEM, VMEM),
        scratch_shapes=[
            pltpu.VMEM((MEMBERS, MEMBERS), jnp.float32),
            pltpu.VMEM((MEMBERS, MEMBERS), jnp.float32),
            pltpu.VMEM((MODES, MEMBERS), jnp.float32),
        ],
        name="factor_and_projection",
    )(stack)


def to_all(values, axes):
    count = lax.axis_size(axes)
    copies = jnp.broadcast_to(values[None], (count,) + values.shape)
    return lax.all_to_all(copies, axes, 0, 0)


def summed(stack):
    axes = ("g", "y")
    count = lax.axis_size(axes)
    pieces = stack.reshape(count, stack.shape[0] // count, LANES)
    piece = lax.all_to_all(pieces, axes, 0, 0).sum(0)
    piece = piece + lax.ppermute(piece, "c", [(0, 1), (1, 0)])
    piece = to_all(piece, "z").sum(0)
    return to_all(piece, axes).reshape(stack.shape)


def body(sensitivity, block_moves, shape_modes):
    panel = sensitivity[0]
    modes = shape_modes[0]
    moves = block_moves[0, 0]
    core = lax.axis_index("c").astype(jnp.int32).reshape(1)
    chain = ("y", "z", "c")
    count = lax.axis_size(chain)
    to_inner, to_outer = parcels(core, moves, panel, modes)
    pairs = range(1, count - 1, 2)
    outer = lax.ppermute(
        to_outer, chain, [(i, i + 1) for i in pairs] + [(i + 1, i) for i in pairs]
    )
    inner = lax.ppermute(to_inner, chain, [(i, i ^ 1) for i in range(count)])
    stack = own_rows(moves, panel, modes)
    stack, near, far = inner_edge(core, moves, panel, modes, inner, stack)
    stack = outer_edge(core, moves, near, far, outer, stack)
    return factor_and_projection(summed(stack))


def solution(mesh):
    split = Mesh(mesh.devices.reshape(4, 8, 2, 4), ("y", "z", "c", "g"))
    spec = P("g", ("y", "z", "c"), None)
    return jax.shard_map(
        body, mesh=split, in_specs=(spec, spec, spec), out_specs=(P(), P()), check_vma=False
    )
```
